128 devices in a mesh: section: 16 (over x_lo, z, core), dp: 8 (over y, x_hi).
Axes of the slice: x: 4 (x_hi: 2, x_lo: 2; x = x_hi * 2 + x_lo), y: 4, z: 4, core: 2. Of those that a mesh axis runs over, the one named last changes fastest.
Arguments:
- in_bases: bfloat16 [16, 8, 10, 24, 8192], P('section', 'dp'), may hold values from -6 to 6
- sent_bases: bfloat16 [16, 8, 10, 24, 8192], P('section', 'dp'), may hold values from -6 to 6
- sample_ids: int32 [8, 8], P('dp'), may hold values from 0 to 9
- exponents: int32 [8, 8, 24, 64], P('dp'), may hold values from -8 to -5
- cotangent: bfloat16 [8, 8, 24, 8192], P('dp'), may hold values from -6 to 6
- w_down: bfloat16 [16, 8192, 256], P('section'), may hold values from -0.0625 to 0.0625
- w_up: bfloat16 [16, 256, 8192], P('section'), may hold values from -0.375 to 0.375
- norm_gain: float32 [16, 8192], P('section'), may hold values from 0.5 to 1.5
Outputs:
- rebuilt: bfloat16 [16, 8, 8, 24, 8192], P('section', 'dp')
- grad_down: float32 [16, 8192, 256], P('section', 'dp')
- grad_up: float32 [16, 256, 8192], P('section', None, 'dp')
- gain_grad: float32 [16, 8192], P('section', 'dp')
The draws below stay inside these ranges and needn't reach their ends.
All inputs are finite; a program needn't handle non-finite values.
Results may differ from the reference program's by a relative error of at most 0.03.
Values may be sent and summed in bfloat16 or wider, within the bound.
A program may use at most 128 MiB of HBM per device.

```python
import jax
import jax.numpy as jnp
from jax import lax

D = 8192
ADAPTER = 256
BLOCK = 128
ROWS = 24
MICRO = 8
SAMPLES = 10
SECTIONS = 16
REPLICAS = 8


def plant(result, own_key, smallest, largest):
    spot = [jax.random.randint(jax.random.fold_in(own_key, axis), (), 0, length) for axis, length in enumerate(result.shape)]
    main_axis = result.shape.index(max(result.shape))
    beside = spot[:main_axis] + [(spot[main_axis] + 1) % result.shape[main_axis]] + spot[main_axis + 1:]
    return result.at[tuple(spot)].set(smallest).at[tuple(beside)].set(largest)


def strengthened(array, rng, source, target, shards_of, factor):
    owner, partner = [(jnp.arange(array.shape[dim]) // (array.shape[dim] // shards_of)).reshape([-1 if axis == dim else 1 for axis in range(array.ndim)]) for dim in (source, target)]
    chosen = jax.random.permutation(rng, shards_of)[partner]
    strong = (owner == chosen) | (owner == (partner + shards_of // 2) % shards_of)
    return jnp.where(strong, factor * array, array)


def block_levels(key, shape, shards, smallest, high):
    factor_of, own = 1.0, jax.random.fold_in(key, 6)
    for dim, shards_of in shards:
        heights = jnp.exp(jax.random.uniform(jax.random.fold_in(own, dim), (shards_of,), jnp.float32, smallest / len(shards), high / len(shards)))
        factor_of = factor_of * jnp.repeat(heights, shape[dim] // shards_of).reshape([-1 if axis == dim else 1 for axis in range(len(shape))])
    return factor_of


def centred(stream_key, shape, deviation, most, split=(), kind=jnp.bfloat16):
    array = deviation * jax.random.normal(stream_key, shape, jnp.float32)
    if split:
        array = array * block_levels(stream_key, shape, split, -0.22, 0.18)
    return jnp.clip(array, -most, most).astype(kind)


def heavy_noise(stream_key, extent, scale, bound, shards, heavy, kind=jnp.bfloat16):
    values = scale * jax.random.normal(stream_key, extent, jnp.float32)
    if shards:
        values = values * block_levels(stream_key, extent, shards, -0.22, 0.18)
    return jnp.clip(strengthened(values, jax.random.fold_in(stream_key, 3), *heavy), -bound, bound).astype(kind)


def setup_inputs(seed: int = 0) -> dict:
    splits = jax.random.split(jax.random.key(seed), 9)
    in_bases = centred(splits[0], (SECTIONS, REPLICAS, SAMPLES, ROWS, D), 1.0, 6.0, ((0, 16), (1, 8)))
    sent_bases = centred(splits[1], (SECTIONS, REPLICAS, SAMPLES, ROWS, D), 1.0, 6.0, ((0, 16), (1, 8)))
    sample_ids = plant(jax.random.randint(splits[2], (REPLICAS, MICRO), 0, SAMPLES), jax.random.fold_in(splits[2], 1), 0, SAMPLES - 1).astype(jnp.int32)
    exponents = plant(jax.random.randint(splits[3], (REPLICAS, MICRO, ROWS, D // BLOCK), -8, -4), jax.random.fold_in(splits[3], 1), -8, (-4) - 1).astype(jnp.int32)
    cotangent = heavy_noise(splits[4], (REPLICAS, MICRO, ROWS, D), 1.0, 6.0, ((0, 8),), (0, 3, 8, 2.0))
    w_down = centred(splits[5], (SECTIONS, D, ADAPTER), D ** -0.5, 0.0625, ((0, 16),))
    w_up = centred(splits[6], (SECTIONS, ADAPTER, D), ADAPTER ** -0.5, 0.375, ((0, 16),))
    norm_gain = jnp.clip(1.0 + 0.1 * jax.random.normal(splits[7], (SECTIONS, D), jnp.float32), 0.5, 1.5)
    return dict(in_bases=in_bases, sent_bases=sent_bases, sample_ids=sample_ids, exponents=exponents, cotangent=cotangent, w_down=w_down, w_up=w_up, norm_gain=norm_gain)


LIMIT = 448.0
EPSILON = 1e-05

def normalize(inputs):
    widened = inputs.astype(jnp.float32)
    spread = jnp.sqrt(lax.optimization_barrier(jnp.mean(widened * widened, axis=-1, keepdims=True)) + EPSILON)
    return (widened / spread, spread)

def dequantize(delta_codes, block_exps):
    shaped = delta_codes.astype(jnp.float32).reshape(delta_codes.shape[:-1] + (D // BLOCK, BLOCK))
    factor = jnp.exp2(block_exps.astype(jnp.float32))[..., None]
    return (shaped * factor).reshape(delta_codes.shape)

def quantize(difference, block_exps):
    shaped = difference.reshape(difference.shape[:-1] + (D // BLOCK, BLOCK))
    factor = jnp.exp2(-block_exps.astype(jnp.float32))[..., None]
    return jnp.clip(shaped * factor, -LIMIT, LIMIT).reshape(difference.shape).astype(jnp.bfloat16)

def layer_forward(inputs, down_proj, up_proj, scale_gain):
    normed, spread = normalize(inputs)
    hidden = (normed * scale_gain).astype(jnp.bfloat16)
    inner = jnp.dot(hidden, down_proj, preferred_element_type=jnp.float32)
    active = jax.nn.silu(inner).astype(jnp.bfloat16)
    output = inputs.astype(jnp.float32) + jnp.dot(active, up_proj, preferred_element_type=jnp.float32)
    return (hidden, inner, active, output)

def layer_backward(grad_out, normed, spread, inner, down_proj, up_proj, scale_gain):
    grad_active = lax.dot_general(grad_out, up_proj, (((1,), (1,)), ((), ())), preferred_element_type=jnp.float32)
    sigma = jax.nn.sigmoid(inner)
    grad_inner = (grad_active * sigma * (1.0 + inner * (1.0 - sigma))).astype(jnp.bfloat16)
    grad_hidden = lax.dot_general(grad_inner, down_proj, (((1,), (1,)), ((), ())), preferred_element_type=jnp.float32)
    gain_terms = lax.optimization_barrier(jnp.sum(grad_hidden * normed, axis=0))
    grad_normed = grad_hidden * scale_gain
    grad_input = grad_out.astype(jnp.float32) + (grad_normed - normed * lax.optimization_barrier(jnp.mean(grad_normed * normed, axis=-1, keepdims=True))) / spread
    return (grad_input.astype(jnp.bfloat16), grad_inner, gain_terms)

def reference(in_bases, sent_bases, sample_ids, exponents, cotangent, w_down, w_up, norm_gain):
    replica_index = jnp.arange(REPLICAS, dtype=jnp.int32)[:, None]
    exps_flat = exponents.reshape(-1, D // BLOCK)

    def forward_section(delta_codes, section_args):
        base_in, base_sent, down_proj, up_proj, scale_gain = section_args
        received = base_in[replica_index, sample_ids].reshape(-1, D)
        sent_copy = base_sent[replica_index, sample_ids].reshape(-1, D)
        rebuilt_now = (received.astype(jnp.float32) + dequantize(delta_codes, exps_flat)).astype(jnp.bfloat16)
        hidden, inner, active, output = layer_forward(rebuilt_now, down_proj, up_proj, scale_gain)
        next_codes = quantize(output - sent_copy.astype(jnp.float32), exps_flat)
        return (next_codes, (rebuilt_now, hidden, inner, active))
    starting = jnp.zeros((REPLICAS * MICRO * ROWS, D), jnp.bfloat16)
    _, stored = lax.scan(forward_section, starting, (in_bases, sent_bases, w_down, w_up, norm_gain))
    rebuilt_all, hidden_all, inner_all, active_all = stored

    def backward_section(grad_out, section_args):
        rebuilt_now, hidden, inner, active, down_proj, up_proj, scale_gain = section_args
        normed, spread = normalize(rebuilt_now)
        grad_input, grad_inner, gain_terms = layer_backward(grad_out, normed, spread, inner, down_proj, up_proj, scale_gain)
        down_terms = jnp.dot(hidden.T, grad_inner, preferred_element_type=jnp.float32)
        up_terms = jnp.dot(active.T, grad_out, preferred_element_type=jnp.float32)
        return (grad_input, (down_terms, up_terms, gain_terms))
    last_grad = cotangent.reshape(-1, D)
    _, grads = lax.scan(backward_section, last_grad, (rebuilt_all, hidden_all, inner_all, active_all, w_down, w_up, norm_gain), reverse=True)
    grad_down, grad_up, gain_grad = grads
    rebuilt = rebuilt_all.reshape(SECTIONS, REPLICAS, MICRO, ROWS, D)
    return (rebuilt, grad_down, grad_up, gain_grad)
```

```python
import functools

import jax
import jax.numpy as jnp
from jax import lax
from jax.experimental import pallas as pl
from jax.experimental.pallas import tpu as pltpu
from jax.sharding import PartitionSpec as P

BLOCK = 128
LIMIT = 448.0
EPSILON = 1e-05
RC = 16
PIECES = 8
MESH = pl.DeviceIdType.MESH
F32 = jnp.float32
BF16 = jnp.bfloat16


def gather_kernel(ids, in_ref, sent_ref, exps_ref, base_ref, copy_ref, lim_ref):
    del ids
    base_ref[...] = in_ref[...]
    copy_ref[...] = sent_ref[...]
    blocks, features = exps_ref.shape[-1], lim_ref.shape[-1]
    bound = (LIMIT * jnp.exp2(exps_ref[0].astype(F32)).astype(BF16).astype(F32)).astype(BF16)
    owner = lax.broadcasted_iota(jnp.int32, (blocks, features), 1) // BLOCK
    row = lax.broadcasted_iota(jnp.int32, (blocks, features), 0)
    spread = jnp.where(owner == row, 1.0, 0.0).astype(BF16)
    lim_ref[0] = jnp.dot(bound, spread, preferred_element_type=F32).astype(BF16)


def gather(ids, in_table, sent_table, exps):
    micro, rows, blocks = exps.shape
    features = in_table.shape[-1]
    picked = pl.BlockSpec((1, rows, features), lambda m, ids: (ids[m], 0, 0))
    placed = pl.BlockSpec((1, rows, features), lambda m, ids: (m, 0, 0))
    shape = jax.ShapeDtypeStruct((micro, rows, features), BF16)
    return pl.pallas_call(
        gather_kernel,
        out_shape=(shape,) * 3,
        grid_spec=pltpu.PrefetchScalarGridSpec(
            num_scalar_prefetch=1,
            grid=(micro,),
            in_specs=[picked, picked, pl.BlockSpec((1, rows, blocks), lambda m, ids: (m, 0, 0))],
            out_specs=(placed,) * 3,
        ),
        compiler_params=pltpu.CompilerParams(vmem_limit_bytes=32 * 2**20),
        name="gather_bases",
    )(ids, in_table, sent_table, exps)


def relay_kernel(
    sections, replicas,
    base_hbm, sent_hbm, lim_hbm, cot_hbm, wd_hbm, wu_hbm, gain,
    reb_hbm, pdown, pup,
    base, delta, sent, lim, go, wd, wu, rb_all, go_all, act_all, gi_all, inner_buf, inv_buf,
    load_sem, f_recv, b_recv, relay_send, x_send, x_recv, out_sem,
):
    s, b = lax.axis_index("section"), lax.axis_index("dp")
    tokens, features = base.shape
    adapter = wd.shape[1]
    chunks = tokens // RC
    width = features // PIECES
    part = features // replicas
    first, last = s == 0, s == sections - 1
    above, below = {"section": s + 1}, {"section": s - 1}

    loads = [
        pltpu.make_async_copy(source, target, load_sem.at[i])
        for i, (source, target) in enumerate(
            [(base_hbm, base), (wd_hbm, wd), (wu_hbm, wu), (sent_hbm, sent), (lim_hbm, lim)]
        )
    ]
    for load in loads:
        load.start()
    cot_load = pltpu.make_async_copy(cot_hbm, go, load_sem.at[5])

    @pl.when(last)
    def _():
        cot_load.start()

    barrier = pltpu.get_barrier_semaphore()

    def greet(device):
        pl.semaphore_signal(barrier, inc=1, device_id=device, device_id_type=MESH)

    @pl.when(jnp.logical_not(first))
    def _():
        greet(below)

    @pl.when(jnp.logical_not(last))
    def _():
        greet(above)

    def peer_of(i):
        return lax.rem(b + 1 + i, replicas)

    def greet_peer(i, _):
        greet({"dp": peer_of(i)})
        return 0

    lax.fori_loop(0, replicas - 1, greet_peer, 0)

    @pl.when(first)
    def _():
        delta[...] = jnp.zeros_like(delta)

    loads[0].wait()
    loads[1].wait()
    pl.semaphore_wait(
        barrier, replicas - 1 + jnp.where(first, 0, 1) + jnp.where(last, 0, 1)
    )

    def exchange(kind, source, target, sem_owner, peer):
        return pltpu.make_async_remote_copy(
            src_ref=source, dst_ref=target,
            send_sem=x_send.at[kind, peer], recv_sem=x_recv.at[kind, sem_owner],
            device_id={"dp": peer}, device_id_type=MESH,
        )

    def relay(forward, chunk, piece):
        rows = pl.ds(pl.multiple_of(chunk * RC, RC), RC)
        cols = pl.ds(pl.multiple_of(piece * width, width), width)
        source, target, recv, way, device = (
            (sent, delta, f_recv, 0, above) if forward else (lim, go, b_recv, 1, below)
        )
        return pltpu.make_async_remote_copy(
            src_ref=source.at[rows, cols], dst_ref=target.at[rows, cols],
            send_sem=relay_send.at[way], recv_sem=recv.at[chunk, piece],
            device_id=device, device_id_type=MESH,
        )

    def forward(chunk):
        rows = pl.ds(pl.multiple_of(chunk * RC, RC), RC)

        def take(k, carry):
            acc, squares = carry
            cols = pl.ds(pl.multiple_of(k * width, width), width)

            @pl.when(jnp.logical_not(first))
            def _():
                relay(True, chunk, k).wait_recv()

            rebuilt = (base[rows, cols].astype(F32) + delta[rows, cols].astype(F32)).astype(BF16)
            base[rows, cols] = rebuilt
            wide = rebuilt.astype(F32)
            square = wide * wide
            for i in range(width // BLOCK):
                squares = squares + square[:, i * BLOCK:(i + 1) * BLOCK]
            hidden = (wide * gain[:, cols]).astype(BF16)
            return acc + jnp.dot(hidden, wd[cols, :], preferred_element_type=F32), squares

        acc, squares = lax.fori_loop(
            0, PIECES, take, (jnp.zeros((RC, adapter), F32), jnp.zeros((RC, BLOCK), F32))
        )
        spread = jnp.sqrt(jnp.sum(squares, axis=1, keepdims=True) / features + EPSILON)
        inverse = 1.0 / spread
        inner = acc * inverse
        active = (inner / (1.0 + jnp.exp(-inner))).astype(BF16)
        inner_buf[rows, :] = inner
        inv_buf[rows, :] = jnp.broadcast_to(inverse, (RC, BLOCK))
        act_all[b, rows, :] = active

        @pl.when(chunk == 0)
        def _():
            for load in loads[2:]:
                load.wait()

        @pl.when(jnp.logical_not(last))
        def _():
            def give(k, _):
                cols = pl.ds(pl.multiple_of(k * width, width), width)
                output = base[rows, cols].astype(F32) + jnp.dot(
                    active, wu[:, cols], preferred_element_type=F32
                )
                bound = lim[rows, cols].astype(F32)
                difference = output - sent[rows, cols].astype(F32)
                sent[rows, cols] = jnp.clip(difference, -bound, bound).astype(BF16)
                relay(True, chunk, k).start()
                return 0

            lax.fori_loop(0, PIECES, give, 0)

        pltpu.make_async_copy(base.at[rows, :], reb_hbm.at[rows, :], out_sem).start()
        rb_all[b, rows, :] = base[rows, pl.ds(pl.multiple_of(b * part, part), part)]

        def share(i, _):
            peer = peer_of(i)
            cols = pl.ds(pl.multiple_of(peer * part, part), part)
            exchange(0, base.at[rows, cols], rb_all.at[b, rows], b, peer).start()
            exchange(1, act_all.at[b, rows], act_all.at[b, rows], b, peer).start()
            return 0

        lax.fori_loop(0, replicas - 1, share, 0)

    def backward(chunk):
        rows = pl.ds(pl.multiple_of(chunk * RC, RC), RC)

        @pl.when(jnp.logical_and(last, chunk == 0))
        def _():
            cot_load.wait()

        def take(k, acc):
            cols = pl.ds(pl.multiple_of(k * width, width), width)

            @pl.when(jnp.logical_not(last))
            def _():
                relay(False, chunk, k).wait_recv()

            return acc + lax.dot_general(
                go[rows, cols], wu[:, cols], (((1,), (1,)), ((), ())), preferred_element_type=F32
            )

        grad_active = lax.fori_loop(0, PIECES, take, jnp.zeros((RC, adapter), F32))
        inner, inverse = inner_buf[rows, :], inv_buf[rows, :][:, :1]
        sigma = 1.0 / (1.0 + jnp.exp(-inner))
        grad_inner = grad_active * sigma * (1.0 + inner * (1.0 - sigma))
        scaled = (grad_inner * inverse).astype(BF16)
        gi_all[b, rows, :] = scaled
        drift = jnp.sum(grad_inner * inner, axis=1, keepdims=True) / features * inverse * inverse

        @pl.when(jnp.logical_not(first))
        def _():
            def give(k, _):
                cols = pl.ds(pl.multiple_of(k * width, width), width)
                grad = lax.dot_general(
                    scaled, wd[cols, :], (((1,), (1,)), ((), ())), preferred_element_type=F32
                )
                lim[rows, cols] = (
                    go[rows, cols].astype(F32)
                    + grad * gain[:, cols]
                    - base[rows, cols].astype(F32) * drift
                ).astype(BF16)
                relay(False, chunk, k).start()
                return 0

            lax.fori_loop(0, PIECES, give, 0)

        go_all[b, rows, :] = go[rows, pl.ds(pl.multiple_of(b * part, part), part)]

        def share(i, _):
            peer = peer_of(i)
            cols = pl.ds(pl.multiple_of(peer * part, part), part)
            exchange(2, go.at[rows, cols], go_all.at[b, rows], b, peer).start()
            exchange(3, gi_all.at[b, rows], gi_all.at[b, rows], b, peer).start()
            return 0

        lax.fori_loop(0, replicas - 1, share, 0)

    def tick(t, _):
        f_chunk = t - s
        b_chunk = t - (2 * sections - 2 - s)

        @pl.when(jnp.logical_and(f_chunk >= 0, f_chunk < chunks))
        def _():
            forward(f_chunk)

        @pl.when(jnp.logical_and(b_chunk >= 0, b_chunk < chunks))
        def _():
            backward(b_chunk)

        return 0

    lax.fori_loop(0, 2 * sections - 2 + chunks, tick, 0)

    def contract(p):
        dims = (((0,), (0,)), ((), ()))
        return (
            lax.dot_general(gi_all[p], rb_all[p], dims, preferred_element_type=F32),
            lax.dot_general(act_all[p], go_all[p], dims, preferred_element_type=F32),
        )

    pdown[...], pup[...] = contract(b)

    def collect(i, _):
        peer = lax.rem(b + replicas - 1 - i, replicas)
        for kind, ref in enumerate((rb_all, act_all, go_all, gi_all)):
            exchange(kind, ref.at[peer], ref.at[peer], peer, peer).wait_recv()
        down, up = contract(peer)
        pdown[...] += down
        pup[...] += up
        return 0

    lax.fori_loop(0, replicas - 1, collect, 0)

    def settle(i, _):
        peer = peer_of(i)
        for kind, ref in enumerate((rb_all, act_all, go_all, gi_all)):
            exchange(kind, ref.at[peer], ref.at[peer], peer, peer).wait_send()
        return 0

    lax.fori_loop(0, replicas - 1, settle, 0)

    def sent_all(buffer, way, device):
        pltpu.make_async_remote_copy(
            src_ref=buffer, dst_ref=buffer, send_sem=relay_send.at[way], recv_sem=f_recv.at[0, 0],
            device_id=device, device_id_type=MESH,
        ).wait_send()

    @pl.when(jnp.logical_not(last))
    def _():
        sent_all(sent, 0, above)

    @pl.when(jnp.logical_not(first))
    def _():
        sent_all(lim, 1, below)

    pltpu.make_async_copy(base, reb_hbm, out_sem).wait()


def relay_call(sections, replicas, base, sent, lim, cotangent, w_down, w_up, gain):
    tokens, features = base.shape
    adapter = w_down.shape[1]
    part = features // replicas
    chunks = tokens // RC
    whole = pltpu.VMEM((tokens, features), BF16)
    anywhere = pl.BlockSpec(memory_space=pl.ANY)
    in_vmem = pl.BlockSpec(memory_space=pltpu.VMEM)
    dma = pltpu.SemaphoreType.DMA
    flops = 12 * tokens * features * adapter
    return pl.pallas_call(
        functools.partial(relay_kernel, sections, replicas),
        out_shape=(
            jax.ShapeDtypeStruct((tokens, features), BF16),
            jax.ShapeDtypeStruct((adapter, part), F32),
            jax.ShapeDtypeStruct((adapter, part), F32),
        ),
        in_specs=[anywhere] * 6 + [in_vmem],
        out_specs=(anywhere, in_vmem, in_vmem),
        scratch_shapes=[
            whole, whole, whole, whole, whole,
            pltpu.VMEM((features, adapter), BF16),
            pltpu.VMEM((adapter, features), BF16),
            pltpu.VMEM((replicas, tokens, part), BF16),
            pltpu.VMEM((replicas, tokens, part), BF16),
            pltpu.VMEM((replicas, tokens, adapter), BF16),
            pltpu.VMEM((replicas, tokens, adapter), BF16),
            pltpu.VMEM((tokens, adapter), F32),
            pltpu.VMEM((tokens, BLOCK), F32),
            dma((6,)), dma((chunks, PIECES)), dma((chunks, PIECES)), dma((2,)),
            dma((4, replicas)), dma((4, replicas)), dma,
        ],
        compiler_params=pltpu.CompilerParams(
            collective_id=0, has_side_effects=True, vmem_limit_bytes=56 * 2**20
        ),
        cost_estimate=pl.CostEstimate(
            flops=flops, bytes_accessed=24 * 2**20, transcendentals=0
        ),
        name="relay",
    )(base, sent, lim, cotangent, w_down, w_up, gain)


def solution(mesh):
    sections, replicas = mesh.shape["section"], mesh.shape["dp"]

    def on_device(in_bases, sent_bases, sample_ids, exponents, cotangent, w_down, w_up, norm_gain):
        micro, rows, features = cotangent.shape[1:]
        tokens = micro * rows
        part = features // replicas
        base, sent, lim = gather(sample_ids[0], in_bases[0, 0], sent_bases[0, 0], exponents[0])
        flat = (tokens, features)
        rebuilt, pdown, pup = relay_call(
            sections, replicas, base.reshape(flat), sent.reshape(flat), lim.reshape(flat),
            cotangent[0].reshape(flat), w_down[0], w_up[0], norm_gain,
        )
        start = lax.axis_index("dp") * part
        gain = lax.dynamic_slice_in_dim(norm_gain[0], start, part, 0)
        down = lax.dynamic_slice_in_dim(w_down[0], start, part, 0)
        plain = pdown.T
        grad_down = plain * gain[:, None]
        gain_grad = jnp.sum(plain * down.astype(F32), axis=1)
        return (
            rebuilt.reshape(1, 1, micro, rows, features),
            grad_down[None],
            pup[None],
            gain_grad[None],
        )

    return jax.shard_map(
        on_device,
        mesh=mesh,
        in_specs=(
            P("section", "dp", None, None, None),
            P("section", "dp", None, None, None),
            P("dp", None),
            P("dp", None, None, None),
            P("dp", None, None, None),
            P("section", None, None),
            P("section", None, None),
            P("section", None),
        ),
        out_specs=(
            P("section", "dp", None, None, None),
            P("section", "dp", None),
            P("section", None, "dp"),
            P("section", "dp"),
        ),
        check_vma=False,
    )
```

```python
import functools

import jax
import jax.numpy as jnp
from jax import lax
from jax.experimental import pallas as pl
from jax.experimental.pallas import tpu as pltpu
from jax.sharding import PartitionSpec as P

BLOCK = 128
LIMIT = 448.0
EPSILON = 1e-05
RC = 16
PIECES = 2
UNIT = 2
GROUPS = 3
MESH = pl.DeviceIdType.MESH
F32 = jnp.float32
BF16 = jnp.bfloat16


def relay_kernel(
    sections, replicas, slab,
    ids, exps_hbm, in_hbm, sent_hbm, cot_hbm, wd_hbm, wu_hbm, gain_hbm,
    reb_hbm, pdown, pup, pgain,
    in_table, sent_table, exps, gain, base, sent, delta, lim, go, zeros, wd, wu, wd_t, wu_t,
    rb_all, go_all, act_all, gi_all, inner_buf, inv_buf,
    load_sem, f_recv, b_recv, relay_send, x_send, x_recv, out_sem,
):
    s, b = lax.axis_index("section"), lax.axis_index("dp")
    tokens, features = base.shape
    adapter = wd.shape[1]
    chunks = tokens // RC
    width = features // PIECES
    part = features // replicas
    per_group = chunks // GROUPS
    first, last = s == 0, s == sections - 1
    above, below = {"section": s + 1}, {"section": s - 1}

    pairs = (
        (exps_hbm, exps), (gain_hbm, gain), (in_hbm, in_table), (wd_hbm, wd),
        (wu_hbm, wu), (sent_hbm, sent_table),
    )
    loads = [
        pltpu.make_async_copy(source, target, load_sem.at[i])
        for i, (source, target) in enumerate(pairs)
    ]
    for load in loads:
        load.start()

    def rows_of(chunk):
        return pl.ds(pl.multiple_of(chunk * RC, RC), RC)

    def cols_of(piece):
        return pl.ds(pl.multiple_of(piece * width, width), width)

    zeros[...] = jnp.zeros_like(zeros)

    @pl.when(first)
    def _():
        def fill(chunk, _):
            for k in range(PIECES):
                pltpu.make_async_copy(
                    zeros, delta.at[rows_of(chunk), cols_of(k)], f_recv.at[chunk, k]
                ).start()
            return 0

        lax.fori_loop(0, chunks, fill, 0)

    @pl.when(last)
    def _():
        def fill(chunk, _):
            for k in range(PIECES):
                block = (rows_of(chunk), cols_of(k))
                pltpu.make_async_copy(
                    cot_hbm.at[block], go.at[block], b_recv.at[chunk, k]
                ).start()
            return 0

        lax.fori_loop(0, chunks, fill, 0)

    barrier = pltpu.get_barrier_semaphore()

    def greet(device):
        pl.semaphore_signal(barrier, inc=1, device_id=device, device_id_type=MESH)

    @pl.when(jnp.logical_not(first))
    def _():
        greet(below)

    @pl.when(jnp.logical_not(last))
    def _():
        greet(above)

    def peer_of(i):
        return lax.rem(b + 1 + i, replicas)

    def greet_peer(i, _):
        greet({"dp": peer_of(i)})
        return 0

    lax.fori_loop(0, replicas - 1, greet_peer, 0)

    loads[0].wait()
    blocks = features // BLOCK
    bound = (LIMIT * jnp.exp2(exps[...].astype(F32)).astype(BF16).astype(F32)).astype(BF16)
    for k in range(PIECES):
        owner = lax.broadcasted_iota(jnp.int32, (blocks, width), 1) // BLOCK + k * (width // BLOCK)
        row = lax.broadcasted_iota(jnp.int32, (blocks, width), 0)
        spread = jnp.where(owner == row, 1.0, 0.0).astype(BF16)
        lim[:, cols_of(k)] = jnp.dot(bound, spread, preferred_element_type=F32).astype(BF16)

    def transpose_weights():
        step = features // 8
        for i in range(8):
            span = pl.ds(i * step, step)
            wd_t[:, span] = wd[span, :].T
            wu_t[span, :] = wu[:, span].T

    shape = (tokens, in_table.shape[0])
    row, column = (lax.broadcasted_iota(jnp.int32, shape, axis) for axis in (0, 1))
    wanted = jnp.zeros(shape, jnp.int32)
    for m in range(tokens // slab):
        inside = jnp.logical_and(row >= m * slab, row < (m + 1) * slab)
        wanted = jnp.where(inside, row + (ids[0, m] - m) * slab, wanted)
    picks = jnp.where(column == wanted, 1.0, 0.0).astype(BF16)

    def pick(table, target):
        step = features // 8

        def some(i, _):
            cols = pl.ds(pl.multiple_of(i * step, step), step)
            target[:, cols] = jnp.dot(
                picks, table[:, cols], preferred_element_type=F32
            ).astype(BF16)
            return 0

        lax.fori_loop(0, 8, some, 0)

    loads[1].wait()
    loads[2].wait()
    pick(in_table, base)

    @pl.when(jnp.logical_not(first))
    def _():
        loads[5].wait()
        pick(sent_table, sent)

    loads[3].wait()
    pl.semaphore_wait(
        barrier, replicas - 1 + jnp.where(first, 0, 1) + jnp.where(last, 0, 1)
    )

    def exchange(kind, source, target, group, owner, peer):
        return pltpu.make_async_remote_copy(
            src_ref=source, dst_ref=target,
            send_sem=x_send.at[kind, peer], recv_sem=x_recv.at[kind, group, owner],
            device_id={"dp": peer}, device_id_type=MESH,
        )

    def relay(forward, chunk, piece):
        block = (rows_of(chunk), cols_of(piece))
        source, target, recv, way, device = (
            (delta, delta, f_recv, 0, above) if forward else (lim, go, b_recv, 1, below)
        )
        return pltpu.make_async_remote_copy(
            src_ref=source.at[block], dst_ref=target.at[block],
            send_sem=relay_send.at[way], recv_sem=recv.at[chunk, piece],
            device_id=device, device_id_type=MESH,
        )

    def place(chunk, count):
        group = chunk // per_group
        offset = pl.multiple_of((chunk % per_group) * RC, RC)
        return group, pl.ds(offset, count * RC)

    def share(kinds, buffer, start, count):
        rows = pl.ds(pl.multiple_of(start * RC, RC), count * RC)
        group, spot = place(start, count)
        wide, narrow = (rb_all, act_all) if kinds == 0 else (go_all, gi_all)

        def to_peer(i, _):
            peer = peer_of(i)
            cols = pl.ds(pl.multiple_of(peer * part, part), part)
            target = wide.at[group, b, spot]
            exchange(kinds, buffer.at[rows, cols], target, group, b, peer).start()
            source = narrow.at[group, b, spot]
            exchange(kinds + 1, source, source, group, b, peer).start()
            return 0

        lax.fori_loop(0, replicas - 1, to_peer, 0)

    def share_forward():
        def one(group, _):
            share(0, base, group * per_group, per_group)
            return 0

        lax.fori_loop(0, GROUPS, one, 0)

    own = pl.ds(pl.multiple_of(b * part, part), part)
    early = s < sections // 4
    pause_mid, pause_end = s < sections // 2, s >= sections * 3 // 4
    within = jnp.logical_not(jnp.logical_or(pause_mid, pause_end))

    def forward(chunk):
        rows = rows_of(chunk)
        group, spot = place(chunk, 1)

        def take(k, carry):
            acc, squares = carry
            cols = cols_of(k)
            relay(True, chunk, k).wait_recv()
            rebuilt = (base[rows, cols].astype(F32) + delta[rows, cols].astype(F32)).astype(BF16)
            base[rows, cols] = rebuilt
            wide = rebuilt.astype(F32)
            square = wide * wide
            for i in range(width // BLOCK):
                squares = squares + square[:, i * BLOCK:(i + 1) * BLOCK]
            hidden = (wide * gain[:, cols]).astype(BF16)
            return acc + jnp.dot(hidden, wd[cols, :], preferred_element_type=F32), squares

        acc, squares = lax.fori_loop(
            0, PIECES, take, (jnp.zeros((RC, adapter), F32), jnp.zeros((RC, BLOCK), F32))
        )
        spread = jnp.sqrt(jnp.sum(squares, axis=1, keepdims=True) / features + EPSILON)
        inverse = 1.0 / spread
        inner = acc * inverse
        active = (inner / (1.0 + jnp.exp(-inner))).astype(BF16)
        inner_buf[rows, :] = inner
        inv_buf[rows, :] = jnp.broadcast_to(inverse, (RC, BLOCK))
        act_all[group, b, spot, :] = active

        @pl.when(jnp.logical_and(chunk == 0, early))
        def _():
            loads[4].wait()

        @pl.when(jnp.logical_and(chunk == 0, first))
        def _():
            loads[5].wait()
            pick(sent_table, sent)

        @pl.when(jnp.logical_not(last))
        def _():
            def give(k, _):
                cols = cols_of(k)
                output = base[rows, cols].astype(F32) + jnp.dot(
                    active, wu[:, cols], preferred_element_type=F32
                )
                bound = lim[rows, cols].astype(F32)
                difference = output - sent[rows, cols].astype(F32)
                delta[rows, cols] = jnp.clip(difference, -bound, bound).astype(BF16)
                relay(True, chunk, k).start()
                return 0

            lax.fori_loop(0, PIECES, give, 0)

        pltpu.make_async_copy(base.at[rows, :], reb_hbm.at[rows, :], out_sem).start()
        rb_all[group, b, spot, :] = base[rows, own]

        @pl.when(jnp.logical_and(within, chunk % UNIT == UNIT - 1))
        def _():
            share(0, base, chunk - (UNIT - 1), UNIT)

    def backward(chunk):
        rows = rows_of(chunk)
        group, spot = place(chunk, 1)

        def take(k, acc):
            cols = cols_of(k)
            relay(False, chunk, k).wait_recv()
            return acc + jnp.dot(go[rows, cols], wu_t[cols, :], preferred_element_type=F32)

        grad_active = lax.fori_loop(0, PIECES, take, jnp.zeros((RC, adapter), F32))
        inner, inverse = inner_buf[rows, :], inv_buf[rows, :][:, :1]
        sigma = 1.0 / (1.0 + jnp.exp(-inner))
        grad_inner = grad_active * sigma * (1.0 + inner * (1.0 - sigma))
        scaled = (grad_inner * inverse).astype(BF16)
        gi_all[group, b, spot, :] = scaled

        @pl.when(jnp.logical_not(first))
        def _():
            drift = (
                jnp.sum(grad_inner * inner, axis=1, keepdims=True) / features * inverse * inverse
            )

            def give(k, _):
                cols = cols_of(k)
                grad = jnp.dot(scaled, wd_t[:, cols], preferred_element_type=F32)
                lim[rows, cols] = (
                    go[rows, cols].astype(F32)
                    + grad * gain[:, cols]
                    - base[rows, cols].astype(F32) * drift
                ).astype(BF16)
                relay(False, chunk, k).start()
                return 0

            lax.fori_loop(0, PIECES, give, 0)

        go_all[group, b, spot, :] = go[rows, own]

        @pl.when(chunk % UNIT == UNIT - 1)
        def _():
            share(2, go, chunk - (UNIT - 1), UNIT)

    def collect(group):
        def arrive(i, _):
            peer = peer_of(i)
            for kind, ref in enumerate((rb_all, act_all, go_all, gi_all)):
                spot = ref.at[group, peer]
                exchange(kind, spot, spot, group, peer, peer).wait_recv()
            return 0

        lax.fori_loop(0, replicas - 1, arrive, 0)
        dims = (((0,), (0,)), ((), ()))
        rows = replicas * per_group * RC
        wide, narrow = (rows, part), (rows, adapter)
        gi_t = gi_all[group].reshape(narrow)
        act_t = act_all[group].reshape(narrow)
        step = part // 2
        for i in range(2):
            cols = pl.ds(i * step, step)
            pdown[:, cols] += lax.dot_general(
                gi_t, rb_all[group, :, :, cols].reshape(rows, step), dims,
                preferred_element_type=F32,
            )
            pup[:, cols] += lax.dot_general(
                act_t, go_all[group, :, :, cols].reshape(rows, step), dims,
                preferred_element_type=F32,
            )

    pdown[...] = jnp.zeros_like(pdown)
    pup[...] = jnp.zeros_like(pup)
    turn_tick = jnp.where(early, chunks - 1 + s, 0)
    spare = s < sections // 2

    def tick(t, _):
        f_chunk = t - s
        b_chunk = t - (2 * sections - 2 - s)

        @pl.when(jnp.logical_and(t == turn_tick, jnp.logical_not(early)))
        def _():
            loads[4].wait()
            transpose_weights()

        @pl.when(jnp.logical_and(f_chunk >= 0, f_chunk < chunks))
        def _():
            forward(f_chunk)

        @pl.when(jnp.logical_and(pause_mid, f_chunk == chunks - 1))
        def _():
            share_forward()

        @pl.when(jnp.logical_and(t == turn_tick, early))
        def _():
            transpose_weights()

        @pl.when(jnp.logical_and(b_chunk >= 0, b_chunk < chunks))
        def _():
            backward(b_chunk)

        for group in range(GROUPS - 1):
            @pl.when(jnp.logical_and(spare, b_chunk == (group + 2) * per_group - 1))
            def _():
                collect(group)

        return 0

    lax.fori_loop(0, 2 * sections - 2 + chunks, tick, 0)

    @pl.when(pause_end)
    def _():
        share_forward()

    def remaining(group, _):
        collect(group)
        return 0

    lax.fori_loop(jnp.where(spare, GROUPS - 1, 0), GROUPS, remaining, 0)
    summed = pdown[...]
    pdown[...] = summed * gain[:, own]
    pgain[...] = jnp.sum(summed * wd_t[:, own].astype(F32), axis=0, keepdims=True)

    def settle(i, _):
        peer = peer_of(i)
        for kind, ref in enumerate((rb_all, act_all, go_all, gi_all)):
            spot = ref.at[:, peer]
            exchange(kind, spot, spot, 0, peer, peer).wait_send()
        return 0

    lax.fori_loop(0, replicas - 1, settle, 0)

    def sent_all(buffer, way, device):
        pltpu.make_async_remote_copy(
            src_ref=buffer, dst_ref=buffer, send_sem=relay_send.at[way], recv_sem=f_recv.at[0, 0],
            device_id=device, device_id_type=MESH,
        ).wait_send()

    @pl.when(jnp.logical_not(last))
    def _():
        sent_all(delta, 0, above)

    @pl.when(jnp.logical_not(first))
    def _():
        sent_all(lim, 1, below)

    pltpu.make_async_copy(base, reb_hbm, out_sem).wait()


def relay_call(sections, replicas, slab, ids, exps, in_table, sent_table, cotangent, w_down, w_up, gain):
    tokens, features = cotangent.shape
    adapter = w_down.shape[1]
    part = features // replicas
    chunks = tokens // RC
    grouped = (GROUPS, replicas, tokens // GROUPS)
    whole = pltpu.VMEM((tokens, features), BF16)
    anywhere = pl.BlockSpec(memory_space=pl.ANY)
    in_vmem = pl.BlockSpec(memory_space=pltpu.VMEM)
    dma = pltpu.SemaphoreType.DMA
    return pl.pallas_call(
        functools.partial(relay_kernel, sections, replicas, slab),
        out_shape=(
            jax.ShapeDtypeStruct((tokens, features), BF16),
            jax.ShapeDtypeStruct((adapter, part), F32),
            jax.ShapeDtypeStruct((adapter, part), F32),
            jax.ShapeDtypeStruct((1, part), F32),
        ),
        in_specs=[pl.BlockSpec(memory_space=pltpu.SMEM)] + [anywhere] * 7,
        out_specs=(anywhere, in_vmem, in_vmem, in_vmem),
        scratch_shapes=[
            pltpu.VMEM(in_table.shape, BF16),
            pltpu.VMEM(sent_table.shape, BF16),
            pltpu.VMEM(exps.shape, jnp.int32),
            pltpu.VMEM((1, features), F32),
            whole, whole, whole, whole, whole,
            pltpu.VMEM((RC, features // PIECES), BF16),
            pltpu.VMEM((features, adapter), BF16),
            pltpu.VMEM((adapter, features), BF16),
            pltpu.VMEM((adapter, features), BF16),
            pltpu.VMEM((features, adapter), BF16),
            pltpu.VMEM(grouped + (part,), BF16),
            pltpu.VMEM(grouped + (part,), BF16),
            pltpu.VMEM(grouped + (adapter,), BF16),
            pltpu.VMEM(grouped + (adapter,), BF16),
            pltpu.VMEM((tokens, adapter), F32),
            pltpu.VMEM((tokens, BLOCK), F32),
            dma((6,)), dma((chunks, PIECES)), dma((chunks, PIECES)), dma((2,)),
            dma((4, replicas)), dma((4, GROUPS, replicas)), dma,
        ],
        compiler_params=pltpu.CompilerParams(
            collective_id=0, has_side_effects=True, vmem_limit_bytes=60 * 2**20
        ),
        cost_estimate=pl.CostEstimate(
            flops=12 * tokens * features * adapter, bytes_accessed=24 * 2**20, transcendentals=0
        ),
        name="relay",
    )(ids, exps, in_table, sent_table, cotangent, w_down, w_up, gain)


def finish_kernel(reb_hbm, pdown, pup, pgain, out_reb, grad_down, grad_up, gain_grad, sems):
    pieces = sems.shape[0]
    step = reb_hbm.shape[0] // pieces
    copies = [
        pltpu.make_async_copy(
            reb_hbm.at[pl.ds(i * step, step)], out_reb.at[pl.ds(i * step, step)], sems.at[i]
        )
        for i in range(pieces)
    ]
    for copy in copies:
        copy.start()
    grad_down[...] = pdown[...].T
    grad_up[...] = pup[...]
    gain_grad[...] = pgain[...]
    for copy in copies:
        copy.wait()


def finish(rebuilt, pdown, pup, pgain):
    anywhere = pl.BlockSpec(memory_space=pl.ANY)
    in_vmem = pl.BlockSpec(memory_space=pltpu.VMEM)
    return pl.pallas_call(
        finish_kernel,
        out_shape=(
            jax.ShapeDtypeStruct(rebuilt.shape, BF16),
            jax.ShapeDtypeStruct(pdown.shape[::-1], F32),
            jax.ShapeDtypeStruct(pup.shape, F32),
            jax.ShapeDtypeStruct(pgain.shape, F32),
        ),
        in_specs=[anywhere, in_vmem, in_vmem, in_vmem],
        out_specs=(anywhere, in_vmem, in_vmem, in_vmem),
        scratch_shapes=[pltpu.SemaphoreType.DMA((6,))],
        compiler_params=pltpu.CompilerParams(vmem_limit_bytes=60 * 2**20),
        name="finish",
    )(rebuilt, pdown, pup, pgain)


def solution(mesh):
    sections, replicas = mesh.shape["section"], mesh.shape["dp"]

    def on_device(in_bases, sent_bases, sample_ids, exponents, cotangent, w_down, w_up, norm_gain):
        micro, rows, features = cotangent.shape[1:]
        flat = (-1, features)
        rebuilt, pdown, pup, pgain = relay_call(
            sections, replicas, rows, sample_ids, exponents[0].reshape(micro * rows, -1),
            in_bases[0, 0].reshape(flat), sent_bases[0, 0].reshape(flat),
            cotangent[0].reshape(flat), w_down[0], w_up[0], norm_gain,
        )
        rebuilt, grad_down, grad_up, gain_grad = finish(rebuilt, pdown, pup, pgain)
        return (
            rebuilt.reshape(1, 1, micro, rows, features),
            grad_down[None],
            grad_up[None],
            gain_grad,
        )

    return jax.shard_map(
        on_device,
        mesh=mesh,
        in_specs=(
            P("section", "dp", None, None, None),
            P("section", "dp", None, None, None),
            P("dp", None),
            P("dp", None, None, None),
            P("dp", None, None, None),
            P("section", None, None),
            P("section", None, None),
            P("section", None),
        ),
        out_specs=(
            P("section", "dp", None, None, None),
            P("section", "dp", None),
            P("section", None, "dp"),
            P("section", "dp"),
        ),
        check_vma=False,
    )
```

```python
import functools

import jax
import jax.numpy as jnp
from jax import lax
from jax.experimental import pallas as pl
from jax.experimental.pallas import tpu as pltpu
from jax.sharding import PartitionSpec as P

BLOCK = 128
LIMIT = 448.0
EPSILON = 1e-05
RC = 16
PIECES = 2
UNIT = 2
LAG_TOP, LAG_BOTTOM = 8, 3
GROUPS = 3
MESH = pl.DeviceIdType.MESH
F32 = jnp.float32
BF16 = jnp.bfloat16


def relay_kernel(
    sections, replicas, slab,
    ids, exps_hbm, in_hbm, sent_hbm, cot_hbm, wd_hbm, wu_hbm, gain_hbm,
    reb_hbm, pdown, pup, pgain,
    in_table, sent_table, exps, gain, base, sent, delta, lim, go, zeros, wd, wu, wd_t, wu_t,
    rb_all, go_all, act_all, gi_all, inner_buf, inv_buf,
    load_sem, f_recv, b_recv, relay_send, x_send, x_recv, out_sem,
):
    s, b = lax.axis_index("section"), lax.axis_index("dp")
    tokens, features = base.shape
    adapter = wd.shape[1]
    chunks = tokens // RC
    width = features // PIECES
    part = features // replicas
    per_group = chunks // GROUPS
    first, last = s == 0, s == sections - 1
    above, below = {"section": s + 1}, {"section": s - 1}

    pairs = (
        (exps_hbm, exps), (gain_hbm, gain), (in_hbm, in_table), (wd_hbm, wd),
        (wu_hbm, wu), (sent_hbm, sent_table),
    )
    loads = [
        pltpu.make_async_copy(source, target, load_sem.at[i])
        for i, (source, target) in enumerate(pairs)
    ]
    for load in loads:
        load.start()

    def rows_of(chunk):
        return pl.ds(pl.multiple_of(chunk * RC, RC), RC)

    def cols_of(piece):
        return pl.ds(pl.multiple_of(piece * width, width), width)

    zeros[...] = jnp.zeros_like(zeros)

    @pl.when(first)
    def _():
        def fill(chunk, _):
            for k in range(PIECES):
                pltpu.make_async_copy(
                    zeros, delta.at[rows_of(chunk), cols_of(k)], f_recv.at[chunk, k]
                ).start()
            return 0

        lax.fori_loop(0, chunks, fill, 0)

    @pl.when(last)
    def _():
        def fill(chunk, _):
            for k in range(PIECES):
                block = (rows_of(chunk), cols_of(k))
                pltpu.make_async_copy(
                    cot_hbm.at[block], go.at[block], b_recv.at[chunk, k]
                ).start()
            return 0

        lax.fori_loop(0, chunks, fill, 0)

    barrier = pltpu.get_barrier_semaphore()

    def greet(device):
        pl.semaphore_signal(barrier, inc=1, device_id=device, device_id_type=MESH)

    @pl.when(jnp.logical_not(first))
    def _():
        greet(below)

    @pl.when(jnp.logical_not(last))
    def _():
        greet(above)

    def peer_of(i):
        return lax.rem(b + 1 + i, replicas)

    def greet_peer(i, _):
        greet({"dp": peer_of(i)})
        return 0

    lax.fori_loop(0, replicas - 1, greet_peer, 0)

    loads[0].wait()
    blocks = features // BLOCK
    bound = (LIMIT * jnp.exp2(exps[...].astype(F32)).astype(BF16).astype(F32)).astype(BF16)
    for k in range(PIECES):
        owner = lax.broadcasted_iota(jnp.int32, (blocks, width), 1) // BLOCK + k * (width // BLOCK)
        row = lax.broadcasted_iota(jnp.int32, (blocks, width), 0)
        spread = jnp.where(owner == row, 1.0, 0.0).astype(BF16)
        lim[:, cols_of(k)] = jnp.dot(bound, spread, preferred_element_type=F32).astype(BF16)

    def transpose_weights():
        step = features // 8
        for i in range(8):
            span = pl.ds(i * step, step)
            wd_t[:, span] = wd[span, :].T
            wu_t[span, :] = wu[:, span].T

    shape = (tokens, in_table.shape[0])
    row, column = (lax.broadcasted_iota(jnp.int32, shape, axis) for axis in (0, 1))
    wanted = jnp.zeros(shape, jnp.int32)
    for m in range(tokens // slab):
        inside = jnp.logical_and(row >= m * slab, row < (m + 1) * slab)
        wanted = jnp.where(inside, row + (ids[0, m] - m) * slab, wanted)
    picks = jnp.where(column == wanted, 1.0, 0.0).astype(BF16)

    def pick(table, target):
        step = features // 8

        def some(i, _):
            cols = pl.ds(pl.multiple_of(i * step, step), step)
            target[:, cols] = jnp.dot(
                picks, table[:, cols], preferred_element_type=F32
            ).astype(BF16)
            return 0

        lax.fori_loop(0, 8, some, 0)

    loads[1].wait()
    loads[2].wait()
    pick(in_table, base)

    @pl.when(jnp.logical_not(first))
    def _():
        loads[5].wait()
        pick(sent_table, sent)

    loads[3].wait()
    pl.semaphore_wait(
        barrier, replicas - 1 + jnp.where(first, 0, 1) + jnp.where(last, 0, 1)
    )

    def exchange(kind, source, target, group, owner, peer):
        return pltpu.make_async_remote_copy(
            src_ref=source, dst_ref=target,
            send_sem=x_send.at[kind, peer], recv_sem=x_recv.at[kind, group, owner],
            device_id={"dp": peer}, device_id_type=MESH,
        )

    def relay(forward, chunk, piece):
        block = (rows_of(chunk), cols_of(piece))
        source, target, recv, way, device = (
            (delta, delta, f_recv, 0, above) if forward else (lim, go, b_recv, 1, below)
        )
        return pltpu.make_async_remote_copy(
            src_ref=source.at[block], dst_ref=target.at[block],
            send_sem=relay_send.at[way], recv_sem=recv.at[chunk, piece],
            device_id=device, device_id_type=MESH,
        )

    def place(chunk, count):
        group = chunk // per_group
        offset = pl.multiple_of((chunk % per_group) * RC, RC)
        return group, pl.ds(offset, count * RC)

    def share(kinds, buffer, start, count):
        rows = pl.ds(pl.multiple_of(start * RC, RC), count * RC)
        group, spot = place(start, count)
        wide, narrow = (rb_all, act_all) if kinds == 0 else (go_all, gi_all)

        def to_peer(i, _):
            peer = peer_of(i)
            cols = pl.ds(pl.multiple_of(peer * part, part), part)
            target = wide.at[group, b, spot]
            exchange(kinds, buffer.at[rows, cols], target, group, b, peer).start()
            source = narrow.at[group, b, spot]
            exchange(kinds + 1, source, source, group, b, peer).start()
            return 0

        lax.fori_loop(0, replicas - 1, to_peer, 0)

    def share_whole(kinds, buffer):
        def one(group, _):
            share(kinds, buffer, group * per_group, per_group)
            return 0

        lax.fori_loop(0, GROUPS, one, 0)

    own = pl.ds(pl.multiple_of(b * part, part), part)
    early = s < sections // 4
    pause_mid, pause_end = s < sections // 2, s >= sections // 2

    def forward(chunk):
        rows = rows_of(chunk)
        group, spot = place(chunk, 1)

        def take(k, carry):
            acc, squares = carry
            cols = cols_of(k)
            relay(True, chunk, k).wait_recv()
            rebuilt = (base[rows, cols].astype(F32) + delta[rows, cols].astype(F32)).astype(BF16)
            base[rows, cols] = rebuilt
            wide = rebuilt.astype(F32)
            square = wide * wide
            for i in range(width // BLOCK):
                squares = squares + square[:, i * BLOCK:(i + 1) * BLOCK]
            hidden = (wide * gain[:, cols]).astype(BF16)
            return acc + jnp.dot(hidden, wd[cols, :], preferred_element_type=F32), squares

        acc, squares = lax.fori_loop(
            0, PIECES, take, (jnp.zeros((RC, adapter), F32), jnp.zeros((RC, BLOCK), F32))
        )
        spread = jnp.sqrt(jnp.sum(squares, axis=1, keepdims=True) / features + EPSILON)
        inverse = 1.0 / spread
        inner = acc * inverse
        active = (inner / (1.0 + jnp.exp(-inner))).astype(BF16)
        inner_buf[rows, :] = inner
        inv_buf[rows, :] = jnp.broadcast_to(inverse, (RC, BLOCK))
        act_all[group, b, spot, :] = active

        @pl.when(jnp.logical_and(chunk == 0, early))
        def _():
            loads[4].wait()

        @pl.when(jnp.logical_and(chunk == 0, first))
        def _():
            loads[5].wait()
            pick(sent_table, sent)

        @pl.when(jnp.logical_not(last))
        def _():
            def give(k, _):
                cols = cols_of(k)
                output = base[rows, cols].astype(F32) + jnp.dot(
                    active, wu[:, cols], preferred_element_type=F32
                )
                bound = lim[rows, cols].astype(F32)
                difference = output - sent[rows, cols].astype(F32)
                delta[rows, cols] = jnp.clip(difference, -bound, bound).astype(BF16)
                relay(True, chunk, k).start()
                return 0

            lax.fori_loop(0, PIECES, give, 0)

        pltpu.make_async_copy(base.at[rows, :], reb_hbm.at[rows, :], out_sem).start()
        rb_all[group, b, spot, :] = base[rows, own]

        @pl.when(jnp.logical_and(jnp.logical_not(pause_mid), chunk % UNIT == UNIT - 1))
        def _():
            share(0, base, chunk - (UNIT - 1), UNIT)

    def backward(chunk):
        rows = rows_of(chunk)
        group, spot = place(chunk, 1)

        def take(k, acc):
            cols = cols_of(k)
            relay(False, chunk, k).wait_recv()
            return acc + jnp.dot(go[rows, cols], wu_t[cols, :], preferred_element_type=F32)

        grad_active = lax.fori_loop(0, PIECES, take, jnp.zeros((RC, adapter), F32))
        inner, inverse = inner_buf[rows, :], inv_buf[rows, :][:, :1]
        sigma = 1.0 / (1.0 + jnp.exp(-inner))
        grad_inner = grad_active * sigma * (1.0 + inner * (1.0 - sigma))
        scaled = (grad_inner * inverse).astype(BF16)
        gi_all[group, b, spot, :] = scaled

        @pl.when(jnp.logical_not(first))
        def _():
            drift = (
                jnp.sum(grad_inner * inner, axis=1, keepdims=True) / features * inverse * inverse
            )

            def give(k, _):
                cols = cols_of(k)
                grad = jnp.dot(scaled, wd_t[:, cols], preferred_element_type=F32)
                lim[rows, cols] = (
                    go[rows, cols].astype(F32)
                    + grad * gain[:, cols]
                    - base[rows, cols].astype(F32) * drift
                ).astype(BF16)
                relay(False, chunk, k).start()
                return 0

            lax.fori_loop(0, PIECES, give, 0)

        go_all[group, b, spot, :] = go[rows, own]

        @pl.when(jnp.logical_and(jnp.logical_not(pause_end), chunk % UNIT == UNIT - 1))
        def _():
            share(2, go, chunk - (UNIT - 1), UNIT)

    def collect(group):
        def arrive(i, _):
            peer = peer_of(i)
            for kind, ref in enumerate((rb_all, act_all, go_all, gi_all)):
                spot = ref.at[group, peer]
                exchange(kind, spot, spot, group, peer, peer).wait_recv()
            return 0

        lax.fori_loop(0, replicas - 1, arrive, 0)
        dims = (((0,), (0,)), ((), ()))
        rows = replicas * per_group * RC
        wide, narrow = (rows, part), (rows, adapter)
        gi_t = gi_all[group].reshape(narrow)
        act_t = act_all[group].reshape(narrow)
        step = part // 2
        for i in range(2):
            cols = pl.ds(i * step, step)
            pdown[:, cols] += lax.dot_general(
                gi_t, rb_all[group, :, :, cols].reshape(rows, step), dims,
                preferred_element_type=F32,
            )
            pup[:, cols] += lax.dot_general(
                act_t, go_all[group, :, :, cols].reshape(rows, step), dims,
                preferred_element_type=F32,
            )

    pdown[...] = jnp.zeros_like(pdown)
    pup[...] = jnp.zeros_like(pup)
    turn_tick = jnp.where(early, chunks - 1, 0)
    lag = (sections - 1 - s) * LAG_TOP // LAG_BOTTOM
    spare = s < sections // 2

    def tick(t, _):
        f_chunk = t
        b_chunk = t - lag

        @pl.when(jnp.logical_and(t == turn_tick, jnp.logical_not(early)))
        def _():
            loads[4].wait()
            transpose_weights()

        @pl.when(f_chunk < chunks)
        def _():
            forward(f_chunk)

        @pl.when(jnp.logical_and(pause_mid, f_chunk == chunks - 1))
        def _():
            share_whole(0, base)

        @pl.when(jnp.logical_and(t == turn_tick, early))
        def _():
            transpose_weights()

        @pl.when(b_chunk >= 0)
        def _():
            backward(b_chunk)

        for group in range(GROUPS - 1):
            @pl.when(jnp.logical_and(spare, b_chunk == (group + 2) * per_group - 1))
            def _():
                collect(group)

        return 0

    lax.fori_loop(0, lag + chunks, tick, 0)

    @pl.when(pause_end)
    def _():
        share_whole(2, go)

    def remaining(group, _):
        collect(group)
        return 0

    lax.fori_loop(jnp.where(spare, GROUPS - 1, 0), GROUPS, remaining, 0)
    summed = pdown[...]
    pdown[...] = summed * gain[:, own]
    pgain[...] = jnp.sum(summed * wd_t[:, own].astype(F32), axis=0, keepdims=True)

    def settle(i, _):
        peer = peer_of(i)
        for kind, ref in enumerate((rb_all, act_all, go_all, gi_all)):
            spot = ref.at[:, peer]
            exchange(kind, spot, spot, 0, peer, peer).wait_send()
        return 0

    lax.fori_loop(0, replicas - 1, settle, 0)

    def sent_all(buffer, way, device):
        pltpu.make_async_remote_copy(
            src_ref=buffer, dst_ref=buffer, send_sem=relay_send.at[way], recv_sem=f_recv.at[0, 0],
            device_id=device, device_id_type=MESH,
        ).wait_send()

    @pl.when(jnp.logical_not(last))
    def _():
        sent_all(delta, 0, above)

    @pl.when(jnp.logical_not(first))
    def _():
        sent_all(lim, 1, below)

    pltpu.make_async_copy(base, reb_hbm, out_sem).wait()


def relay_call(sections, replicas, slab, ids, exps, in_table, sent_table, cotangent, w_down, w_up, gain):
    tokens, features = cotangent.shape
    adapter = w_down.shape[1]
    part = features // replicas
    chunks = tokens // RC
    grouped = (GROUPS, replicas, tokens // GROUPS)
    whole = pltpu.VMEM((tokens, features), BF16)
    anywhere = pl.BlockSpec(memory_space=pl.ANY)
    in_vmem = pl.BlockSpec(memory_space=pltpu.VMEM)
    dma = pltpu.SemaphoreType.DMA
    return pl.pallas_call(
        functools.partial(relay_kernel, sections, replicas, slab),
        out_shape=(
            jax.ShapeDtypeStruct((tokens, features), BF16),
            jax.ShapeDtypeStruct((adapter, part), F32),
            jax.ShapeDtypeStruct((adapter, part), F32),
            jax.ShapeDtypeStruct((1, part), F32),
        ),
        in_specs=[pl.BlockSpec(memory_space=pltpu.SMEM)] + [anywhere] * 7,
        out_specs=(anywhere, in_vmem, in_vmem, in_vmem),
        scratch_shapes=[
            pltpu.VMEM(in_table.shape, BF16),
            pltpu.VMEM(sent_table.shape, BF16),
            pltpu.VMEM(exps.shape, jnp.int32),
            pltpu.VMEM((1, features), F32),
            whole, whole, whole, whole, whole,
            pltpu.VMEM((RC, features // PIECES), BF16),
            pltpu.VMEM((features, adapter), BF16),
            pltpu.VMEM((adapter, features), BF16),
            pltpu.VMEM((adapter, features), BF16),
            pltpu.VMEM((features, adapter), BF16),
            pltpu.VMEM(grouped + (part,), BF16),
            pltpu.VMEM(grouped + (part,), BF16),
            pltpu.VMEM(grouped + (adapter,), BF16),
            pltpu.VMEM(grouped + (adapter,), BF16),
            pltpu.VMEM((tokens, adapter), F32),
            pltpu.VMEM((tokens, BLOCK), F32),
            dma((6,)), dma((chunks, PIECES)), dma((chunks, PIECES)), dma((2,)),
            dma((4, replicas)), dma((4, GROUPS, replicas)), dma,
        ],
        compiler_params=pltpu.CompilerParams(
            collective_id=0, has_side_effects=True, vmem_limit_bytes=60 * 2**20
        ),
        cost_estimate=pl.CostEstimate(
            flops=12 * tokens * features * adapter, bytes_accessed=24 * 2**20, transcendentals=0
        ),
        name="relay",
    )(ids, exps, in_table, sent_table, cotangent, w_down, w_up, gain)


def finish_kernel(reb, pdown, pup, pgain, out_reb, grad_down, grad_up, gain_grad):
    out_reb[...] = reb[...]
    grad_down[...] = pdown[...].T
    grad_up[...] = pup[...]
    gain_grad[...] = pgain[...]


def finish(rebuilt, pdown, pup, pgain):
    steps = 4
    (tokens, features), (adapter, part) = rebuilt.shape, pdown.shape
    block = pl.BlockSpec((tokens // steps, features), lambda i: (i, 0))
    across = pl.BlockSpec((adapter, part // steps), lambda i: (0, i))
    down = pl.BlockSpec((part // steps, adapter), lambda i: (i, 0))
    gains = pl.BlockSpec((1, part // steps), lambda i: (0, i))
    return pl.pallas_call(
        finish_kernel,
        out_shape=(
            jax.ShapeDtypeStruct(rebuilt.shape, BF16),
            jax.ShapeDtypeStruct((part, adapter), F32),
            jax.ShapeDtypeStruct(pup.shape, F32),
            jax.ShapeDtypeStruct(pgain.shape, F32),
        ),
        grid=(steps,),
        in_specs=[block, across, across, gains],
        out_specs=(block, down, across, gains),
        compiler_params=pltpu.CompilerParams(vmem_limit_bytes=60 * 2**20),
        name="finish",
    )(rebuilt, pdown, pup, pgain)


def solution(mesh):
    sections, replicas = mesh.shape["section"], mesh.shape["dp"]

    def on_device(in_bases, sent_bases, sample_ids, exponents, cotangent, w_down, w_up, norm_gain):
        micro, rows, features = cotangent.shape[1:]
        flat = (-1, features)
        rebuilt, pdown, pup, pgain = relay_call(
            sections, replicas, rows, sample_ids, exponents[0].reshape(micro * rows, -1),
            in_bases[0, 0].reshape(flat), sent_bases[0, 0].reshape(flat),
            cotangent[0].reshape(flat), w_down[0], w_up[0], norm_gain,
        )
        rebuilt, grad_down, grad_up, gain_grad = finish(rebuilt, pdown, pup, pgain)
        return (
            rebuilt.reshape(1, 1, micro, rows, features),
            grad_down[None],
            grad_up[None],
            gain_grad,
        )

    return jax.shard_map(
        on_device,
        mesh=mesh,
        in_specs=(
            P("section", "dp", None, None, None),
            P("section", "dp", None, None, None),
            P("dp", None),
            P("dp", None, None, None),
            P("dp", None, None, None),
            P("section", None, None),
            P("section", None, None),
            P("section", None),
        ),
        out_specs=(
            P("section", "dp", None, None, None),
            P("section", "dp", None),
            P("section", None, "dp"),
            P("section", "dp"),
        ),
        check_vma=False,
    )
```

```python
import functools

import jax
import jax.numpy as jnp
from jax import lax
from jax.experimental import pallas as pl
from jax.experimental.pallas import tpu as pltpu
from jax.sharding import PartitionSpec as P

BLOCK = 128
LIMIT = 448.0
EPSILON = 1e-05
RC = 16
PIECES = 2
UNIT = 1
LAG_TOP, LAG_BOTTOM = 8, 3
GROUPS = 3
MESH = pl.DeviceIdType.MESH
F32 = jnp.float32
BF16 = jnp.bfloat16


def relay_kernel(
    sections, replicas, slab,
    ids, exps_hbm, in_hbm, sent_hbm, cot_hbm, wd_hbm, wu_hbm, gain_hbm,
    reb_hbm, pdown, pup, pgain,
    in_table, sent_table, exps, gain, base, sent, delta, lim, go, zeros, wd, wu, wd_t, wu_t,
    rb_all, go_all, act_all, gi_all, inner_buf, inv_buf,
    load_sem, f_recv, b_recv, relay_send, x_send, x_recv, out_sem,
):
    s, b = lax.axis_index("section"), lax.axis_index("dp")
    tokens, features = base.shape
    adapter = wd.shape[1]
    chunks = tokens // RC
    width = features // PIECES
    part = features // replicas
    per_group = chunks // GROUPS
    first, last = s == 0, s == sections - 1
    above, below = {"section": s + 1}, {"section": s - 1}

    pairs = (
        (exps_hbm, exps), (gain_hbm, gain), (in_hbm, in_table), (wd_hbm, wd),
        (wu_hbm, wu), (sent_hbm, sent_table),
    )
    loads = [
        pltpu.make_async_copy(source, target, load_sem.at[i])
        for i, (source, target) in enumerate(pairs)
    ]
    for load in loads:
        load.start()

    def rows_of(chunk):
        return pl.ds(pl.multiple_of(chunk * RC, RC), RC)

    def cols_of(piece):
        return pl.ds(pl.multiple_of(piece * width, width), width)

    zeros[...] = jnp.zeros_like(zeros)

    @pl.when(first)
    def _():
        def fill(chunk, _):
            for k in range(PIECES):
                pltpu.make_async_copy(
                    zeros, delta.at[rows_of(chunk), cols_of(k)], f_recv.at[chunk, k]
                ).start()
            return 0

        lax.fori_loop(0, chunks, fill, 0)

    @pl.when(last)
    def _():
        def fill(chunk, _):
            for k in range(PIECES):
                block = (rows_of(chunk), cols_of(k))
                pltpu.make_async_copy(
                    cot_hbm.at[block], go.at[block], b_recv.at[chunk, k]
                ).start()
            return 0

        lax.fori_loop(0, chunks, fill, 0)

    barrier = pltpu.get_barrier_semaphore()

    def greet(device):
        pl.semaphore_signal(barrier, inc=1, device_id=device, device_id_type=MESH)

    @pl.when(jnp.logical_not(first))
    def _():
        greet(below)

    @pl.when(jnp.logical_not(last))
    def _():
        greet(above)

    def peer_of(i):
        return lax.rem(b + 1 + i, replicas)

    def greet_peer(i, _):
        greet({"dp": peer_of(i)})
        return 0

    lax.fori_loop(0, replicas - 1, greet_peer, 0)

    loads[0].wait()
    blocks = features // BLOCK
    bound = (LIMIT * jnp.exp2(exps[...].astype(F32)).astype(BF16).astype(F32)).astype(BF16)
    for k in range(PIECES):
        owner = lax.broadcasted_iota(jnp.int32, (blocks, width), 1) // BLOCK + k * (width // BLOCK)
        row = lax.broadcasted_iota(jnp.int32, (blocks, width), 0)
        spread = jnp.where(owner == row, 1.0, 0.0).astype(BF16)
        lim[:, cols_of(k)] = jnp.dot(bound, spread, preferred_element_type=F32).astype(BF16)

    def transpose_weights():
        step = features // 8
        for i in range(8):
            span = pl.ds(i * step, step)
            wd_t[:, span] = wd[span, :].T
            wu_t[span, :] = wu[:, span].T

    shape = (tokens, in_table.shape[0])
    row, column = (lax.broadcasted_iota(jnp.int32, shape, axis) for axis in (0, 1))
    wanted = jnp.zeros(shape, jnp.int32)
    for m in range(tokens // slab):
        inside = jnp.logical_and(row >= m * slab, row < (m + 1) * slab)
        wanted = jnp.where(inside, row + (ids[0, m] - m) * slab, wanted)
    picks = jnp.where(column == wanted, 1.0, 0.0).astype(BF16)

    def pick(table, target):
        step = features // 8

        def some(i, _):
            cols = pl.ds(pl.multiple_of(i * step, step), step)
            target[:, cols] = jnp.dot(
                picks, table[:, cols], preferred_element_type=F32
            ).astype(BF16)
            return 0

        lax.fori_loop(0, 8, some, 0)

    loads[1].wait()
    loads[2].wait()
    pick(in_table, base)

    @pl.when(jnp.logical_not(first))
    def _():
        loads[5].wait()
        pick(sent_table, sent)

    loads[3].wait()
    pl.semaphore_wait(
        barrier, replicas - 1 + jnp.where(first, 0, 1) + jnp.where(last, 0, 1)
    )

    def exchange(kind, source, target, group, owner, peer):
        return pltpu.make_async_remote_copy(
            src_ref=source, dst_ref=target,
            send_sem=x_send.at[kind, peer], recv_sem=x_recv.at[kind, group, owner],
            device_id={"dp": peer}, device_id_type=MESH,
        )

    def relay(forward, chunk, piece):
        block = (rows_of(chunk), cols_of(piece))
        source, target, recv, way, device = (
            (delta, delta, f_recv, 0, above) if forward else (lim, go, b_recv, 1, below)
        )
        return pltpu.make_async_remote_copy(
            src_ref=source.at[block], dst_ref=target.at[block],
            send_sem=relay_send.at[way], recv_sem=recv.at[chunk, piece],
            device_id=device, device_id_type=MESH,
        )

    def place(chunk, count):
        group = chunk // per_group
        offset = pl.multiple_of((chunk % per_group) * RC, RC)
        return group, pl.ds(offset, count * RC)

    def share(kinds, buffer, start, count):
        rows = pl.ds(pl.multiple_of(start * RC, RC), count * RC)
        group, spot = place(start, count)
        wide, narrow = (rb_all, act_all) if kinds == 0 else (go_all, gi_all)

        def to_peer(i, _):
            peer = peer_of(i)
            cols = pl.ds(pl.multiple_of(peer * part, part), part)
            target = wide.at[group, b, spot]
            exchange(kinds, buffer.at[rows, cols], target, group, b, peer).start()
            source = narrow.at[group, b, spot]
            exchange(kinds + 1, source, source, group, b, peer).start()
            return 0

        lax.fori_loop(0, replicas - 1, to_peer, 0)

    def share_whole(kinds, buffer):
        def one(group, _):
            share(kinds, buffer, group * per_group, per_group)
            return 0

        lax.fori_loop(0, GROUPS, one, 0)

    own = pl.ds(pl.multiple_of(b * part, part), part)
    early = s < sections // 4
    pause_mid, pause_end = s < sections // 2, s >= sections // 2

    def forward(chunk):
        rows = rows_of(chunk)
        group, spot = place(chunk, 1)

        def take(k, carry):
            acc, squares = carry
            cols = cols_of(k)
            relay(True, chunk, k).wait_recv()
            rebuilt = (base[rows, cols].astype(F32) + delta[rows, cols].astype(F32)).astype(BF16)
            base[rows, cols] = rebuilt
            wide = rebuilt.astype(F32)
            square = wide * wide
            for i in range(width // BLOCK):
                squares = squares + square[:, i * BLOCK:(i + 1) * BLOCK]
            hidden = (wide * gain[:, cols]).astype(BF16)
            return acc + jnp.dot(hidden, wd[cols, :], preferred_element_type=F32), squares

        acc, squares = lax.fori_loop(
            0, PIECES, take, (jnp.zeros((RC, adapter), F32), jnp.zeros((RC, BLOCK), F32))
        )
        spread = jnp.sqrt(jnp.sum(squares, axis=1, keepdims=True) / features + EPSILON)
        inverse = 1.0 / spread
        inner = acc * inverse
        active = (inner / (1.0 + jnp.exp(-inner))).astype(BF16)
        inner_buf[rows, :] = inner
        inv_buf[rows, :] = jnp.broadcast_to(inverse, (RC, BLOCK))
        act_all[group, b, spot, :] = active

        @pl.when(jnp.logical_and(chunk == 0, early))
        def _():
            loads[4].wait()

        @pl.when(jnp.logical_and(chunk == 0, first))
        def _():
            loads[5].wait()
            pick(sent_table, sent)

        @pl.when(jnp.logical_not(last))
        def _():
            def give(k, _):
                cols = cols_of(k)
                output = base[rows, cols].astype(F32) + jnp.dot(
                    active, wu[:, cols], preferred_element_type=F32
                )
                bound = lim[rows, cols].astype(F32)
                difference = output - sent[rows, cols].astype(F32)
                delta[rows, cols] = jnp.clip(difference, -bound, bound).astype(BF16)
                relay(True, chunk, k).start()
                return 0

            lax.fori_loop(0, PIECES, give, 0)

        pltpu.make_async_copy(base.at[rows, :], reb_hbm.at[rows, :], out_sem).start()
        rb_all[group, b, spot, :] = base[rows, own]

        @pl.when(jnp.logical_and(jnp.logical_not(pause_mid), chunk % UNIT == UNIT - 1))
        def _():
            share(0, base, chunk - (UNIT - 1), UNIT)

    def backward(chunk):
        rows = rows_of(chunk)
        group, spot = place(chunk, 1)

        def take(k, acc):
            cols = cols_of(k)
            relay(False, chunk, k).wait_recv()
            return acc + jnp.dot(go[rows, cols], wu_t[cols, :], preferred_element_type=F32)

        grad_active = lax.fori_loop(0, PIECES, take, jnp.zeros((RC, adapter), F32))
        inner, inverse = inner_buf[rows, :], inv_buf[rows, :][:, :1]
        sigma = 1.0 / (1.0 + jnp.exp(-inner))
        grad_inner = grad_active * sigma * (1.0 + inner * (1.0 - sigma))
        scaled = (grad_inner * inverse).astype(BF16)
        gi_all[group, b, spot, :] = scaled

        @pl.when(jnp.logical_not(first))
        def _():
            drift = (
                jnp.sum(grad_inner * inner, axis=1, keepdims=True) / features * inverse * inverse
            )

            def give(k, _):
                cols = cols_of(k)
                grad = jnp.dot(scaled, wd_t[:, cols], preferred_element_type=F32)
                lim[rows, cols] = (
                    go[rows, cols].astype(F32)
                    + grad * gain[:, cols]
                    - base[rows, cols].astype(F32) * drift
                ).astype(BF16)
                relay(False, chunk, k).start()
                return 0

            lax.fori_loop(0, PIECES, give, 0)

        go_all[group, b, spot, :] = go[rows, own]

        @pl.when(jnp.logical_and(jnp.logical_not(pause_end), chunk % UNIT == UNIT - 1))
        def _():
            share(2, go, chunk - (UNIT - 1), UNIT)

    def collect(group):
        def arrive(i, _):
            peer = peer_of(i)
            for kind, ref in enumerate((rb_all, act_all, go_all, gi_all)):
                spot = ref.at[group, peer]
                exchange(kind, spot, spot, group, peer, peer).wait_recv()
            return 0

        lax.fori_loop(0, replicas - 1, arrive, 0)
        dims = (((0,), (0,)), ((), ()))
        rows = replicas * per_group * RC
        wide, narrow = (rows, part), (rows, adapter)
        gi_t = gi_all[group].reshape(narrow)
        act_t = act_all[group].reshape(narrow)
        step = part // 2
        for i in range(2):
            cols = pl.ds(i * step, step)
            pdown[:, cols] += lax.dot_general(
                gi_t, rb_all[group, :, :, cols].reshape(rows, step), dims,
                preferred_element_type=F32,
            )
            pup[:, cols] += lax.dot_general(
                act_t, go_all[group, :, :, cols].reshape(rows, step), dims,
                preferred_element_type=F32,
            )

    pdown[...] = jnp.zeros_like(pdown)
    pup[...] = jnp.zeros_like(pup)
    turn_tick = jnp.where(early, chunks - 1, 0)
    lag = (sections - 1 - s) * LAG_TOP // LAG_BOTTOM
    spare = s < sections // 2

    def tick(t, _):
        f_chunk = t
        b_chunk = t - lag

        @pl.when(jnp.logical_and(t == turn_tick, jnp.logical_not(early)))
        def _():
            loads[4].wait()
            transpose_weights()

        @pl.when(f_chunk < chunks)
        def _():
            forward(f_chunk)

        @pl.when(jnp.logical_and(pause_mid, f_chunk == chunks - 1))
        def _():
            share_whole(0, base)

        @pl.when(jnp.logical_and(t == turn_tick, early))
        def _():
            transpose_weights()

        @pl.when(b_chunk >= 0)
        def _():
            backward(b_chunk)

        for group in range(GROUPS - 1):
            @pl.when(jnp.logical_and(spare, b_chunk == (group + 2) * per_group - 1))
            def _():
                collect(group)

        return 0

    lax.fori_loop(0, lag + chunks, tick, 0)

    @pl.when(pause_end)
    def _():
        share_whole(2, go)

    def remaining(group, _):
        collect(group)
        return 0

    lax.fori_loop(jnp.where(spare, GROUPS - 1, 0), GROUPS, remaining, 0)
    summed = pdown[...]
    pdown[...] = summed * gain[:, own]
    pgain[...] = jnp.sum(summed * wd_t[:, own].astype(F32), axis=0, keepdims=True)

    def settle(i, _):
        peer = peer_of(i)
        for kind, ref in enumerate((rb_all, act_all, go_all, gi_all)):
            spot = ref.at[:, peer]
            exchange(kind, spot, spot, 0, peer, peer).wait_send()
        return 0

    lax.fori_loop(0, replicas - 1, settle, 0)

    def sent_all(buffer, way, device):
        pltpu.make_async_remote_copy(
            src_ref=buffer, dst_ref=buffer, send_sem=relay_send.at[way], recv_sem=f_recv.at[0, 0],
            device_id=device, device_id_type=MESH,
        ).wait_send()

    @pl.when(jnp.logical_not(last))
    def _():
        sent_all(delta, 0, above)

    @pl.when(jnp.logical_not(first))
    def _():
        sent_all(lim, 1, below)

    pltpu.make_async_copy(base, reb_hbm, out_sem).wait()


def relay_call(sections, replicas, slab, ids, exps, in_table, sent_table, cotangent, w_down, w_up, gain):
    tokens, features = cotangent.shape
    adapter = w_down.shape[1]
    part = features // replicas
    chunks = tokens // RC
    grouped = (GROUPS, replicas, tokens // GROUPS)
    whole = pltpu.VMEM((tokens, features), BF16)
    anywhere = pl.BlockSpec(memory_space=pl.ANY)
    in_vmem = pl.BlockSpec(memory_space=pltpu.VMEM)
    dma = pltpu.SemaphoreType.DMA
    return pl.pallas_call(
        functools.partial(relay_kernel, sections, replicas, slab),
        out_shape=(
            jax.ShapeDtypeStruct((tokens, features), BF16),
            jax.ShapeDtypeStruct((adapter, part), F32),
            jax.ShapeDtypeStruct((adapter, part), F32),
            jax.ShapeDtypeStruct((1, part), F32),
        ),
        in_specs=[pl.BlockSpec(memory_space=pltpu.SMEM)] + [anywhere] * 7,
        out_specs=(anywhere, in_vmem, in_vmem, in_vmem),
        scratch_shapes=[
            pltpu.VMEM(in_table.shape, BF16),
            pltpu.VMEM(sent_table.shape, BF16),
            pltpu.VMEM(exps.shape, jnp.int32),
            pltpu.VMEM((1, features), F32),
            whole, whole, whole, whole, whole,
            pltpu.VMEM((RC, features // PIECES), BF16),
            pltpu.VMEM((features, adapter), BF16),
            pltpu.VMEM((adapter, features), BF16),
            pltpu.VMEM((adapter, features), BF16),
            pltpu.VMEM((features, adapter), BF16),
            pltpu.VMEM(grouped + (part,), BF16),
            pltpu.VMEM(grouped + (part,), BF16),
            pltpu.VMEM(grouped + (adapter,), BF16),
            pltpu.VMEM(grouped + (adapter,), BF16),
            pltpu.VMEM((tokens, adapter), F32),
            pltpu.VMEM((tokens, BLOCK), F32),
            dma((6,)), dma((chunks, PIECES)), dma((chunks, PIECES)), dma((2,)),
            dma((4, replicas)), dma((4, GROUPS, replicas)), dma,
        ],
        compiler_params=pltpu.CompilerParams(
            collective_id=0, has_side_effects=True, vmem_limit_bytes=60 * 2**20
        ),
        cost_estimate=pl.CostEstimate(
            flops=12 * tokens * features * adapter, bytes_accessed=24 * 2**20, transcendentals=0
        ),
        name="relay",
    )(ids, exps, in_table, sent_table, cotangent, w_down, w_up, gain)


def finish_kernel(reb, pdown, pup, pgain, out_reb, grad_down, grad_up, gain_grad):
    out_reb[...] = reb[...]
    grad_down[...] = pdown[...].T
    grad_up[...] = pup[...]
    gain_grad[...] = pgain[...]


def finish(rebuilt, pdown, pup, pgain):
    steps = 2
    (tokens, features), (adapter, part) = rebuilt.shape, pdown.shape
    block = pl.BlockSpec((tokens // steps, features), lambda i: (i, 0))
    across = pl.BlockSpec((adapter, part // steps), lambda i: (0, i))
    down = pl.BlockSpec((part // steps, adapter), lambda i: (i, 0))
    gains = pl.BlockSpec((1, part // steps), lambda i: (0, i))
    return pl.pallas_call(
        finish_kernel,
        out_shape=(
            jax.ShapeDtypeStruct(rebuilt.shape, BF16),
            jax.ShapeDtypeStruct((part, adapter), F32),
            jax.ShapeDtypeStruct(pup.shape, F32),
            jax.ShapeDtypeStruct(pgain.shape, F32),
        ),
        grid=(steps,),
        in_specs=[block, across, across, gains],
        out_specs=(block, down, across, gains),
        compiler_params=pltpu.CompilerParams(vmem_limit_bytes=60 * 2**20),
        name="finish",
    )(rebuilt, pdown, pup, pgain)


def solution(mesh):
    sections, replicas = mesh.shape["section"], mesh.shape["dp"]

    def on_device(in_bases, sent_bases, sample_ids, exponents, cotangent, w_down, w_up, norm_gain):
        micro, rows, features = cotangent.shape[1:]
        flat = (-1, features)
        rebuilt, pdown, pup, pgain = relay_call(
            sections, replicas, rows, sample_ids, exponents[0].reshape(micro * rows, -1),
            in_bases[0, 0].reshape(flat), sent_bases[0, 0].reshape(flat),
            cotangent[0].reshape(flat), w_down[0], w_up[0], norm_gain,
        )
        rebuilt, grad_down, grad_up, gain_grad = finish(rebuilt, pdown, pup, pgain)
        return (
            rebuilt.reshape(1, 1, micro, rows, features),
            grad_down[None],
            grad_up[None],
            gain_grad,
        )

    return jax.shard_map(
        on_device,
        mesh=mesh,
        in_specs=(
            P("section", "dp", None, None, None),
            P("section", "dp", None, None, None),
            P("dp", None),
            P("dp", None, None, None),
            P("dp", None, None, None),
            P("section", None, None),
            P("section", None, None),
            P("section", None),
        ),
        out_specs=(
            P("section", "dp", None, None, None),
            P("section", "dp", None),
            P("section", None, "dp"),
            P("section", "dp"),
        ),
        check_vma=False,
    )
```

```python
import functools

import jax
import jax.numpy as jnp
from jax import lax
from jax.experimental import pallas as pl
from jax.experimental.pallas import tpu as pltpu
from jax.sharding import PartitionSpec as P

BLOCK = 128
LIMIT = 448.0
EPSILON = 1e-05
RC = 16
PIECES = 2
UNIT = 1
LAG_TOP, LAG_BOTTOM = 8, 3
PROMPT = 2
GROUPS = 3
MESH = pl.DeviceIdType.MESH
F32 = jnp.float32
BF16 = jnp.bfloat16


def relay_kernel(
    sections, replicas, slab,
    ids, exps_hbm, in_hbm, sent_hbm, cot_hbm, wd_hbm, wu_hbm, gain_hbm,
    reb_hbm, pdown, pup, pgain,
    in_table, sent_table, exps, gain, base, sent, delta, lim, go, zeros, wd, wu, wd_t, wu_t,
    rb_all, go_all, act_all, gi_all, inner_buf, inv_buf,
    load_sem, f_recv, b_recv, relay_send, x_send, x_recv, out_sem,
):
    s, b = lax.axis_index("section"), lax.axis_index("dp")
    tokens, features = base.shape
    adapter = wd.shape[1]
    chunks = tokens // RC
    width = features // PIECES
    part = features // replicas
    per_group = chunks // GROUPS
    first, last = s == 0, s == sections - 1
    above, below = {"section": s + 1}, {"section": s - 1}

    pairs = (
        (exps_hbm, exps), (gain_hbm, gain), (in_hbm, in_table), (wd_hbm, wd),
        (wu_hbm, wu), (sent_hbm, sent_table),
    )
    loads = [
        pltpu.make_async_copy(source, target, load_sem.at[i])
        for i, (source, target) in enumerate(pairs)
    ]
    for load in loads:
        load.start()

    def rows_of(chunk):
        return pl.ds(pl.multiple_of(chunk * RC, RC), RC)

    def cols_of(piece):
        return pl.ds(pl.multiple_of(piece * width, width), width)

    zeros[...] = jnp.zeros_like(zeros)

    @pl.when(first)
    def _():
        def fill(chunk, _):
            for k in range(PIECES):
                pltpu.make_async_copy(
                    zeros, delta.at[rows_of(chunk), cols_of(k)], f_recv.at[chunk, k]
                ).start()
            return 0

        lax.fori_loop(0, chunks, fill, 0)

    @pl.when(last)
    def _():
        def fill(chunk, _):
            for k in range(PIECES):
                block = (rows_of(chunk), cols_of(k))
                pltpu.make_async_copy(
                    cot_hbm.at[block], go.at[block], b_recv.at[chunk, k]
                ).start()
            return 0

        lax.fori_loop(0, chunks, fill, 0)

    barrier = pltpu.get_barrier_semaphore()

    def greet(device):
        pl.semaphore_signal(barrier, inc=1, device_id=device, device_id_type=MESH)

    @pl.when(jnp.logical_not(first))
    def _():
        greet(below)

    @pl.when(jnp.logical_not(last))
    def _():
        greet(above)

    def peer_of(i):
        return lax.rem(b + 1 + i, replicas)

    def greet_peer(i, _):
        greet({"dp": peer_of(i)})
        return 0

    lax.fori_loop(0, replicas - 1, greet_peer, 0)

    loads[0].wait()
    blocks = features // BLOCK
    bound = (LIMIT * jnp.exp2(exps[...].astype(F32)).astype(BF16).astype(F32)).astype(BF16)
    for k in range(PIECES):
        owner = lax.broadcasted_iota(jnp.int32, (blocks, width), 1) // BLOCK + k * (width // BLOCK)
        row = lax.broadcasted_iota(jnp.int32, (blocks, width), 0)
        spread = jnp.where(owner == row, 1.0, 0.0).astype(BF16)
        lim[:, cols_of(k)] = jnp.dot(bound, spread, preferred_element_type=F32).astype(BF16)

    def transpose_weights():
        step = features // 8
        for i in range(8):
            span = pl.ds(i * step, step)
            wd_t[:, span] = wd[span, :].T
            wu_t[span, :] = wu[:, span].T

    shape = (tokens, in_table.shape[0])
    row, column = (lax.broadcasted_iota(jnp.int32, shape, axis) for axis in (0, 1))
    wanted = jnp.zeros(shape, jnp.int32)
    for m in range(tokens // slab):
        inside = jnp.logical_and(row >= m * slab, row < (m + 1) * slab)
        wanted = jnp.where(inside, row + (ids[0, m] - m) * slab, wanted)
    picks = jnp.where(column == wanted, 1.0, 0.0).astype(BF16)

    def pick(table, target):
        step = features // 8

        def some(i, _):
            cols = pl.ds(pl.multiple_of(i * step, step), step)
            target[:, cols] = jnp.dot(
                picks, table[:, cols], preferred_element_type=F32
            ).astype(BF16)
            return 0

        lax.fori_loop(0, 8, some, 0)

    loads[1].wait()
    loads[2].wait()
    pick(in_table, base)

    @pl.when(jnp.logical_not(first))
    def _():
        loads[5].wait()
        pick(sent_table, sent)

    loads[3].wait()
    pl.semaphore_wait(
        barrier, replicas - 1 + jnp.where(first, 0, 1) + jnp.where(last, 0, 1)
    )

    def exchange(kind, source, target, group, owner, peer):
        return pltpu.make_async_remote_copy(
            src_ref=source, dst_ref=target,
            send_sem=x_send.at[kind, peer], recv_sem=x_recv.at[kind, group, owner],
            device_id={"dp": peer}, device_id_type=MESH,
        )

    def relay(forward, chunk, piece):
        block = (rows_of(chunk), cols_of(piece))
        source, target, recv, way, device = (
            (delta, delta, f_recv, 0, above) if forward else (lim, go, b_recv, 1, below)
        )
        return pltpu.make_async_remote_copy(
            src_ref=source.at[block], dst_ref=target.at[block],
            send_sem=relay_send.at[way], recv_sem=recv.at[chunk, piece],
            device_id=device, device_id_type=MESH,
        )

    def place(chunk, count):
        group = chunk // per_group
        offset = pl.multiple_of((chunk % per_group) * RC, RC)
        return group, pl.ds(offset, count * RC)

    def share(kinds, buffer, start, count):
        rows = pl.ds(pl.multiple_of(start * RC, RC), count * RC)
        group, spot = place(start, count)
        wide, narrow = (rb_all, act_all) if kinds == 0 else (go_all, gi_all)

        def to_peer(i, _):
            peer = peer_of(i)
            cols = pl.ds(pl.multiple_of(peer * part, part), part)
            target = wide.at[group, b, spot]
            exchange(kinds, buffer.at[rows, cols], target, group, b, peer).start()
            source = narrow.at[group, b, spot]
            exchange(kinds + 1, source, source, group, b, peer).start()
            return 0

        lax.fori_loop(0, replicas - 1, to_peer, 0)

    def share_whole(kinds, buffer, start):
        def one(group, _):
            share(kinds, buffer, group * per_group, per_group)
            return 0

        lax.fori_loop(start, GROUPS, one, 0)

    own = pl.ds(pl.multiple_of(b * part, part), part)
    early = s < sections // 4
    pause_mid, pause_end = s < sections // 2, s >= sections // 2
    prompt = jnp.where(s >= sections * 3 // 4, PROMPT, GROUPS)

    def forward(chunk):
        rows = rows_of(chunk)
        group, spot = place(chunk, 1)

        def take(k, carry):
            acc, squares = carry
            cols = cols_of(k)
            relay(True, chunk, k).wait_recv()
            rebuilt = (base[rows, cols].astype(F32) + delta[rows, cols].astype(F32)).astype(BF16)
            base[rows, cols] = rebuilt
            wide = rebuilt.astype(F32)
            square = wide * wide
            for i in range(width // BLOCK):
                squares = squares + square[:, i * BLOCK:(i + 1) * BLOCK]
            hidden = (wide * gain[:, cols]).astype(BF16)
            return acc + jnp.dot(hidden, wd[cols, :], preferred_element_type=F32), squares

        acc, squares = lax.fori_loop(
            0, PIECES, take, (jnp.zeros((RC, adapter), F32), jnp.zeros((RC, BLOCK), F32))
        )
        spread = jnp.sqrt(jnp.sum(squares, axis=1, keepdims=True) / features + EPSILON)
        inverse = 1.0 / spread
        inner = acc * inverse
        active = (inner / (1.0 + jnp.exp(-inner))).astype(BF16)
        inner_buf[rows, :] = inner
        inv_buf[rows, :] = jnp.broadcast_to(inverse, (RC, BLOCK))
        act_all[group, b, spot, :] = active

        @pl.when(jnp.logical_and(chunk == 0, early))
        def _():
            loads[4].wait()

        @pl.when(jnp.logical_and(chunk == 0, first))
        def _():
            loads[5].wait()
            pick(sent_table, sent)

        @pl.when(jnp.logical_not(last))
        def _():
            def give(k, _):
                cols = cols_of(k)
                output = base[rows, cols].astype(F32) + jnp.dot(
                    active, wu[:, cols], preferred_element_type=F32
                )
                bound = lim[rows, cols].astype(F32)
                difference = output - sent[rows, cols].astype(F32)
                delta[rows, cols] = jnp.clip(difference, -bound, bound).astype(BF16)
                relay(True, chunk, k).start()
                return 0

            lax.fori_loop(0, PIECES, give, 0)

        pltpu.make_async_copy(base.at[rows, :], reb_hbm.at[rows, :], out_sem).start()
        rb_all[group, b, spot, :] = base[rows, own]

        @pl.when(pause_end & (chunk < prompt * per_group) & (chunk % UNIT == UNIT - 1))
        def _():
            share(0, base, chunk - (UNIT - 1), UNIT)

    def backward(chunk):
        rows = rows_of(chunk)
        group, spot = place(chunk, 1)

        def take(k, acc):
            cols = cols_of(k)
            relay(False, chunk, k).wait_recv()
            return acc + jnp.dot(go[rows, cols], wu_t[cols, :], preferred_element_type=F32)

        grad_active = lax.fori_loop(0, PIECES, take, jnp.zeros((RC, adapter), F32))
        inner, inverse = inner_buf[rows, :], inv_buf[rows, :][:, :1]
        sigma = 1.0 / (1.0 + jnp.exp(-inner))
        grad_inner = grad_active * sigma * (1.0 + inner * (1.0 - sigma))
        scaled = (grad_inner * inverse).astype(BF16)
        gi_all[group, b, spot, :] = scaled

        @pl.when(jnp.logical_not(first))
        def _():
            drift = (
                jnp.sum(grad_inner * inner, axis=1, keepdims=True) / features * inverse * inverse
            )

            def give(k, _):
                cols = cols_of(k)
                grad = jnp.dot(scaled, wd_t[:, cols], preferred_element_type=F32)
                lim[rows, cols] = (
                    go[rows, cols].astype(F32)
                    + grad * gain[:, cols]
                    - base[rows, cols].astype(F32) * drift
                ).astype(BF16)
                relay(False, chunk, k).start()
                return 0

            lax.fori_loop(0, PIECES, give, 0)

        go_all[group, b, spot, :] = go[rows, own]

        @pl.when(jnp.logical_and(jnp.logical_not(pause_end), chunk % UNIT == UNIT - 1))
        def _():
            share(2, go, chunk - (UNIT - 1), UNIT)

    def collect(group):
        def arrive(i, _):
            peer = peer_of(i)
            for kind, ref in enumerate((rb_all, act_all, go_all, gi_all)):
                spot = ref.at[group, peer]
                exchange(kind, spot, spot, group, peer, peer).wait_recv()
            return 0

        lax.fori_loop(0, replicas - 1, arrive, 0)
        dims = (((0,), (0,)), ((), ()))
        rows = replicas * per_group * RC
        wide, narrow = (rows, part), (rows, adapter)
        gi_t = gi_all[group].reshape(narrow)
        act_t = act_all[group].reshape(narrow)
        step = part // 2
        for i in range(2):
            cols = pl.ds(i * step, step)
            pdown[:, cols] += lax.dot_general(
                gi_t, rb_all[group, :, :, cols].reshape(rows, step), dims,
                preferred_element_type=F32,
            )
            pup[:, cols] += lax.dot_general(
                act_t, go_all[group, :, :, cols].reshape(rows, step), dims,
                preferred_element_type=F32,
            )

    pdown[...] = jnp.zeros_like(pdown)
    pup[...] = jnp.zeros_like(pup)
    turn_tick = jnp.where(early, chunks - 1, 0)
    lag = (sections - 1 - s) * LAG_TOP // LAG_BOTTOM
    spare = s < sections // 2

    def tick(t, _):
        f_chunk = t
        b_chunk = t - lag

        @pl.when(jnp.logical_and(t == turn_tick, jnp.logical_not(early)))
        def _():
            loads[4].wait()
            transpose_weights()

        @pl.when(f_chunk < chunks)
        def _():
            forward(f_chunk)

        @pl.when(jnp.logical_and(pause_mid, f_chunk == chunks - 1))
        def _():
            share_whole(0, base, 0)

        @pl.when(jnp.logical_and(t == turn_tick, early))
        def _():
            transpose_weights()

        @pl.when(b_chunk >= 0)
        def _():
            backward(b_chunk)

        for group in range(GROUPS - 1):
            @pl.when(jnp.logical_and(spare, b_chunk == (group + 2) * per_group - 1))
            def _():
                collect(group)

        return 0

    lax.fori_loop(0, lag + chunks, tick, 0)

    @pl.when(pause_end)
    def _():
        share_whole(0, base, prompt)
        share_whole(2, go, 0)

    def remaining(group, _):
        collect(group)
        return 0

    lax.fori_loop(jnp.where(spare, GROUPS - 1, 0), GROUPS, remaining, 0)
    summed = pdown[...]
    pdown[...] = summed * gain[:, own]
    pgain[...] = jnp.sum(summed * wd_t[:, own].astype(F32), axis=0, keepdims=True)

    def settle(i, _):
        peer = peer_of(i)
        for kind, ref in enumerate((rb_all, act_all, go_all, gi_all)):
            spot = ref.at[:, peer]
            exchange(kind, spot, spot, 0, peer, peer).wait_send()
        return 0

    lax.fori_loop(0, replicas - 1, settle, 0)

    def sent_all(buffer, way, device):
        pltpu.make_async_remote_copy(
            src_ref=buffer, dst_ref=buffer, send_sem=relay_send.at[way], recv_sem=f_recv.at[0, 0],
            device_id=device, device_id_type=MESH,
        ).wait_send()

    @pl.when(jnp.logical_not(last))
    def _():
        sent_all(delta, 0, above)

    @pl.when(jnp.logical_not(first))
    def _():
        sent_all(lim, 1, below)

    pltpu.make_async_copy(base, reb_hbm, out_sem).wait()


def relay_call(sections, replicas, slab, ids, exps, in_table, sent_table, cotangent, w_down, w_up, gain):
    tokens, features = cotangent.shape
    adapter = w_down.shape[1]
    part = features // replicas
    chunks = tokens // RC
    grouped = (GROUPS, replicas, tokens // GROUPS)
    whole = pltpu.VMEM((tokens, features), BF16)
    anywhere = pl.BlockSpec(memory_space=pl.ANY)
    in_vmem = pl.BlockSpec(memory_space=pltpu.VMEM)
    dma = pltpu.SemaphoreType.DMA
    return pl.pallas_call(
        functools.partial(relay_kernel, sections, replicas, slab),
        out_shape=(
            jax.ShapeDtypeStruct((tokens, features), BF16),
            jax.ShapeDtypeStruct((adapter, part), F32),
            jax.ShapeDtypeStruct((adapter, part), F32),
            jax.ShapeDtypeStruct((1, part), F32),
        ),
        in_specs=[pl.BlockSpec(memory_space=pltpu.SMEM)] + [anywhere] * 7,
        out_specs=(anywhere, in_vmem, in_vmem, in_vmem),
        scratch_shapes=[
            pltpu.VMEM(in_table.shape, BF16),
            pltpu.VMEM(sent_table.shape, BF16),
            pltpu.VMEM(exps.shape, jnp.int32),
            pltpu.VMEM((1, features), F32),
            whole, whole, whole, whole, whole,
            pltpu.VMEM((RC, features // PIECES), BF16),
            pltpu.VMEM((features, adapter), BF16),
            pltpu.VMEM((adapter, features), BF16),
            pltpu.VMEM((adapter, features), BF16),
            pltpu.VMEM((features, adapter), BF16),
            pltpu.VMEM(grouped + (part,), BF16),
            pltpu.VMEM(grouped + (part,), BF16),
            pltpu.VMEM(grouped + (adapter,), BF16),
            pltpu.VMEM(grouped + (adapter,), BF16),
            pltpu.VMEM((tokens, adapter), F32),
            pltpu.VMEM((tokens, BLOCK), F32),
            dma((6,)), dma((chunks, PIECES)), dma((chunks, PIECES)), dma((2,)),
            dma((4, replicas)), dma((4, GROUPS, replicas)), dma,
        ],
        compiler_params=pltpu.CompilerParams(
            collective_id=0, has_side_effects=True, vmem_limit_bytes=60 * 2**20
        ),
        cost_estimate=pl.CostEstimate(
            flops=12 * tokens * features * adapter, bytes_accessed=24 * 2**20, transcendentals=0
        ),
        name="relay",
    )(ids, exps, in_table, sent_table, cotangent, w_down, w_up, gain)


def finish_kernel(reb, pdown, pup, pgain, out_reb, grad_down, grad_up, gain_grad):
    out_reb[...] = reb[...]
    grad_down[...] = pdown[...].T
    grad_up[...] = pup[...]
    gain_grad[...] = pgain[...]


def finish(rebuilt, pdown, pup, pgain):
    steps = 2
    (tokens, features), (adapter, part) = rebuilt.shape, pdown.shape
    block = pl.BlockSpec((tokens // steps, features), lambda i: (i, 0))
    across = pl.BlockSpec((adapter, part // steps), lambda i: (0, i))
    down = pl.BlockSpec((part // steps, adapter), lambda i: (i, 0))
    gains = pl.BlockSpec((1, part // steps), lambda i: (0, i))
    return pl.pallas_call(
        finish_kernel,
        out_shape=(
            jax.ShapeDtypeStruct(rebuilt.shape, BF16),
            jax.ShapeDtypeStruct((part, adapter), F32),
            jax.ShapeDtypeStruct(pup.shape, F32),
            jax.ShapeDtypeStruct(pgain.shape, F32),
        ),
        grid=(steps,),
        in_specs=[block, across, across, gains],
        out_specs=(block, down, across, gains),
        compiler_params=pltpu.CompilerParams(vmem_limit_bytes=60 * 2**20),
        name="finish",
    )(rebuilt, pdown, pup, pgain)


def solution(mesh):
    sections, replicas = mesh.shape["section"], mesh.shape["dp"]

    def on_device(in_bases, sent_bases, sample_ids, exponents, cotangent, w_down, w_up, norm_gain):
        micro, rows, features = cotangent.shape[1:]
        flat = (-1, features)
        rebuilt, pdown, pup, pgain = relay_call(
            sections, replicas, rows, sample_ids, exponents[0].reshape(micro * rows, -1),
            in_bases[0, 0].reshape(flat), sent_bases[0, 0].reshape(flat),
            cotangent[0].reshape(flat), w_down[0], w_up[0], norm_gain,
        )
        rebuilt, grad_down, grad_up, gain_grad = finish(rebuilt, pdown, pup, pgain)
        return (
            rebuilt.reshape(1, 1, micro, rows, features),
            grad_down[None],
            grad_up[None],
            gain_grad,
        )

    return jax.shard_map(
        on_device,
        mesh=mesh,
        in_specs=(
            P("section", "dp", None, None, None),
            P("section", "dp", None, None, None),
            P("dp", None),
            P("dp", None, None, None),
            P("dp", None, None, None),
            P("section", None, None),
            P("section", None, None),
            P("section", None),
        ),
        out_specs=(
            P("section", "dp", None, None, None),
            P("section", "dp", None),
            P("section", None, "dp"),
            P("section", "dp"),
        ),
        check_vma=False,
    )
```

```python
import functools

import jax
import jax.numpy as jnp
from jax import lax
from jax.experimental import pallas as pl
from jax.experimental.pallas import tpu as pltpu
from jax.sharding import PartitionSpec as P

BLOCK = 128
LIMIT = 448.0
EPSILON = 1e-05
RC = 16
PIECES = 2
UNIT = 1
LAG_TOP, LAG_BOTTOM = 8, 3
GROUPS = 3
MESH = pl.DeviceIdType.MESH
F32 = jnp.float32
BF16 = jnp.bfloat16


def relay_kernel(
    sections, replicas, slab,
    ids, exps_hbm, in_hbm, sent_hbm, cot_hbm, wd_hbm, wu_hbm, gain_hbm,
    reb_hbm, pdown, pup, pgain,
    in_table, sent_table, exps, gain, base, sent, delta, lim, go, zeros, wd, wu, wd_t, wu_t,
    rb_all, go_all, act_all, gi_all, inner_buf, inv_buf,
    load_sem, f_recv, b_recv, relay_send, x_send, x_recv, out_sem,
):
    s, b = lax.axis_index("section"), lax.axis_index("dp")
    tokens, features = base.shape
    adapter = wd.shape[1]
    chunks = tokens // RC
    width = features // PIECES
    part = features // replicas
    per_group = chunks // GROUPS
    first, last = s == 0, s == sections - 1
    above, below = {"section": s + 1}, {"section": s - 1}

    pairs = (
        (exps_hbm, exps), (gain_hbm, gain), (in_hbm, in_table), (wd_hbm, wd),
        (wu_hbm, wu), (sent_hbm, sent_table),
    )
    loads = [
        pltpu.make_async_copy(source, target, load_sem.at[i])
        for i, (source, target) in enumerate(pairs)
    ]
    for load in loads:
        load.start()

    def rows_of(chunk):
        return pl.ds(pl.multiple_of(chunk * RC, RC), RC)

    def cols_of(piece):
        return pl.ds(pl.multiple_of(piece * width, width), width)

    zeros[...] = jnp.zeros_like(zeros)

    @pl.when(first)
    def _():
        def fill(chunk, _):
            for k in range(PIECES):
                pltpu.make_async_copy(
                    zeros, delta.at[rows_of(chunk), cols_of(k)], f_recv.at[chunk, k]
                ).start()
            return 0

        lax.fori_loop(0, chunks, fill, 0)

    @pl.when(last)
    def _():
        def fill(chunk, _):
            for k in range(PIECES):
                block = (rows_of(chunk), cols_of(k))
                pltpu.make_async_copy(
                    cot_hbm.at[block], go.at[block], b_recv.at[chunk, k]
                ).start()
            return 0

        lax.fori_loop(0, chunks, fill, 0)

    barrier = pltpu.get_barrier_semaphore()

    def greet(device):
        pl.semaphore_signal(barrier, inc=1, device_id=device, device_id_type=MESH)

    @pl.when(jnp.logical_not(first))
    def _():
        greet(below)

    @pl.when(jnp.logical_not(last))
    def _():
        greet(above)

    def peer_of(i):
        return lax.rem(b + 1 + i, replicas)

    def greet_peer(i, _):
        greet({"dp": peer_of(i)})
        return 0

    lax.fori_loop(0, replicas - 1, greet_peer, 0)

    loads[0].wait()
    blocks = features // BLOCK
    bound = (LIMIT * jnp.exp2(exps[...].astype(F32)).astype(BF16).astype(F32)).astype(BF16)
    for k in range(PIECES):
        owner = lax.broadcasted_iota(jnp.int32, (blocks, width), 1) // BLOCK + k * (width // BLOCK)
        row = lax.broadcasted_iota(jnp.int32, (blocks, width), 0)
        spread = jnp.where(owner == row, 1.0, 0.0).astype(BF16)
        lim[:, cols_of(k)] = jnp.dot(bound, spread, preferred_element_type=F32).astype(BF16)

    def transpose_weights():
        step = features // 8
        for i in range(8):
            span = pl.ds(i * step, step)
            wd_t[:, span] = wd[span, :].T
            wu_t[span, :] = wu[:, span].T

    shape = (tokens, in_table.shape[0])
    row, column = (lax.broadcasted_iota(jnp.int32, shape, axis) for axis in (0, 1))
    wanted = jnp.zeros(shape, jnp.int32)
    for m in range(tokens // slab):
        inside = jnp.logical_and(row >= m * slab, row < (m + 1) * slab)
        wanted = jnp.where(inside, row + (ids[0, m] - m) * slab, wanted)
    picks = jnp.where(column == wanted, 1.0, 0.0).astype(BF16)

    def pick(table, target):
        step = features // 8

        def some(i, _):
            cols = pl.ds(pl.multiple_of(i * step, step), step)
            target[:, cols] = jnp.dot(
                picks, table[:, cols], preferred_element_type=F32
            ).astype(BF16)
            return 0

        lax.fori_loop(0, 8, some, 0)

    loads[1].wait()
    loads[2].wait()
    pick(in_table, base)

    @pl.when(jnp.logical_not(first))
    def _():
        loads[5].wait()
        pick(sent_table, sent)

    loads[3].wait()
    pl.semaphore_wait(
        barrier, replicas - 1 + jnp.where(first, 0, 1) + jnp.where(last, 0, 1)
    )

    def exchange(kind, source, target, group, owner, peer):
        return pltpu.make_async_remote_copy(
            src_ref=source, dst_ref=target,
            send_sem=x_send.at[kind, peer], recv_sem=x_recv.at[kind, group, owner],
            device_id={"dp": peer}, device_id_type=MESH,
        )

    def relay(forward, chunk, piece):
        block = (rows_of(chunk), cols_of(piece))
        source, target, recv, way, device = (
            (delta, delta, f_recv, 0, above) if forward else (lim, go, b_recv, 1, below)
        )
        return pltpu.make_async_remote_copy(
            src_ref=source.at[block], dst_ref=target.at[block],
            send_sem=relay_send.at[way], recv_sem=recv.at[chunk, piece],
            device_id=device, device_id_type=MESH,
        )

    def place(chunk, count):
        group = chunk // per_group
        offset = pl.multiple_of((chunk % per_group) * RC, RC)
        return group, pl.ds(offset, count * RC)

    def share(kinds, buffer, start, count):
        rows = pl.ds(pl.multiple_of(start * RC, RC), count * RC)
        group, spot = place(start, count)
        wide, narrow = (rb_all, act_all) if kinds == 0 else (go_all, gi_all)

        def to_peer(i, _):
            peer = peer_of(i)
            cols = pl.ds(pl.multiple_of(peer * part, part), part)
            target = wide.at[group, b, spot]
            exchange(kinds, buffer.at[rows, cols], target, group, b, peer).start()
            source = narrow.at[group, b, spot]
            exchange(kinds + 1, source, source, group, b, peer).start()
            return 0

        lax.fori_loop(0, replicas - 1, to_peer, 0)

    def share_whole(kinds, buffer):
        def one(group, _):
            share(kinds, buffer, group * per_group, per_group)
            return 0

        lax.fori_loop(0, GROUPS, one, 0)

    own = pl.ds(pl.multiple_of(b * part, part), part)
    early = s < sections // 4
    pause_mid, pause_end = s < sections // 2, s >= sections // 2

    def forward(chunk):
        rows = rows_of(chunk)
        group, spot = place(chunk, 1)

        def take(k, carry):
            acc, squares = carry
            cols = cols_of(k)
            relay(True, chunk, k).wait_recv()
            rebuilt = (base[rows, cols].astype(F32) + delta[rows, cols].astype(F32)).astype(BF16)
            base[rows, cols] = rebuilt
            wide = rebuilt.astype(F32)
            square = wide * wide
            for i in range(width // BLOCK):
                squares = squares + square[:, i * BLOCK:(i + 1) * BLOCK]
            hidden = (wide * gain[:, cols]).astype(BF16)
            return acc + jnp.dot(hidden, wd[cols, :], preferred_element_type=F32), squares

        acc, squares = lax.fori_loop(
            0, PIECES, take, (jnp.zeros((RC, adapter), F32), jnp.zeros((RC, BLOCK), F32))
        )
        spread = jnp.sqrt(jnp.sum(squares, axis=1, keepdims=True) / features + EPSILON)
        inverse = 1.0 / spread
        inner = acc * inverse
        active = (inner / (1.0 + jnp.exp(-inner))).astype(BF16)
        inner_buf[rows, :] = inner
        inv_buf[rows, :] = jnp.broadcast_to(inverse, (RC, BLOCK))
        act_all[group, b, spot, :] = active

        @pl.when(jnp.logical_and(chunk == 0, early))
        def _():
            loads[4].wait()

        @pl.when(jnp.logical_and(chunk == 0, first))
        def _():
            loads[5].wait()
            pick(sent_table, sent)

        @pl.when(jnp.logical_not(last))
        def _():
            def give(k, _):
                cols = cols_of(k)
                output = base[rows, cols].astype(F32) + jnp.dot(
                    active, wu[:, cols], preferred_element_type=F32
                )
                bound = lim[rows, cols].astype(F32)
                difference = output - sent[rows, cols].astype(F32)
                delta[rows, cols] = jnp.clip(difference, -bound, bound).astype(BF16)
                relay(True, chunk, k).start()
                return 0

            lax.fori_loop(0, PIECES, give, 0)

        pltpu.make_async_copy(base.at[rows, :], reb_hbm.at[rows, :], out_sem).start()
        rb_all[group, b, spot, :] = base[rows, own]

        @pl.when(jnp.logical_and(jnp.logical_not(pause_mid), chunk % 2 == 1))
        def _():
            share(0, base, chunk - 1, 2)

    def backward(chunk):
        rows = rows_of(chunk)
        group, spot = place(chunk, 1)

        def take(k, acc):
            cols = cols_of(k)
            relay(False, chunk, k).wait_recv()
            return acc + jnp.dot(go[rows, cols], wu_t[cols, :], preferred_element_type=F32)

        grad_active = lax.fori_loop(0, PIECES, take, jnp.zeros((RC, adapter), F32))
        inner, inverse = inner_buf[rows, :], inv_buf[rows, :][:, :1]
        sigma = 1.0 / (1.0 + jnp.exp(-inner))
        grad_inner = grad_active * sigma * (1.0 + inner * (1.0 - sigma))
        scaled = (grad_inner * inverse).astype(BF16)
        gi_all[group, b, spot, :] = scaled

        @pl.when(jnp.logical_not(first))
        def _():
            drift = (
                jnp.sum(grad_inner * inner, axis=1, keepdims=True) / features * inverse * inverse
            )

            def give(k, _):
                cols = cols_of(k)
                grad = jnp.dot(scaled, wd_t[:, cols], preferred_element_type=F32)
                lim[rows, cols] = (
                    go[rows, cols].astype(F32)
                    + grad * gain[:, cols]
                    - base[rows, cols].astype(F32) * drift
                ).astype(BF16)
                relay(False, chunk, k).start()
                return 0

            lax.fori_loop(0, PIECES, give, 0)

        go_all[group, b, spot, :] = go[rows, own]

        @pl.when(jnp.logical_and(jnp.logical_not(pause_end), chunk % UNIT == UNIT - 1))
        def _():
            share(2, go, chunk - (UNIT - 1), UNIT)

    def collect(group):
        def arrive(i, _):
            peer = peer_of(i)
            for kind, ref in enumerate((rb_all, act_all, go_all, gi_all)):
                spot = ref.at[group, peer]
                exchange(kind, spot, spot, group, peer, peer).wait_recv()
            return 0

        lax.fori_loop(0, replicas - 1, arrive, 0)
        dims = (((0,), (0,)), ((), ()))
        rows = replicas * per_group * RC
        wide, narrow = (rows, part), (rows, adapter)
        gi_t = gi_all[group].reshape(narrow)
        act_t = act_all[group].reshape(narrow)
        step = part // 2
        for i in range(2):
            cols = pl.ds(i * step, step)
            pdown[:, cols] += lax.dot_general(
                gi_t, rb_all[group, :, :, cols].reshape(rows, step), dims,
                preferred_element_type=F32,
            )
            pup[:, cols] += lax.dot_general(
                act_t, go_all[group, :, :, cols].reshape(rows, step), dims,
                preferred_element_type=F32,
            )

    pdown[...] = jnp.zeros_like(pdown)
    pup[...] = jnp.zeros_like(pup)
    turn_tick = jnp.where(early, chunks - 1, 0)
    lag = (sections - 1 - s) * LAG_TOP // LAG_BOTTOM
    spare = s < sections // 2

    def tick(t, _):
        f_chunk = t
        b_chunk = t - lag

        @pl.when(jnp.logical_and(t == turn_tick, jnp.logical_not(early)))
        def _():
            loads[4].wait()
            transpose_weights()

        @pl.when(f_chunk < chunks)
        def _():
            forward(f_chunk)

        @pl.when(jnp.logical_and(pause_mid, f_chunk == chunks - 1))
        def _():
            share_whole(0, base)

        @pl.when(jnp.logical_and(t == turn_tick, early))
        def _():
            transpose_weights()

        @pl.when(b_chunk >= 0)
        def _():
            backward(b_chunk)

        for group in range(GROUPS - 1):
            @pl.when(jnp.logical_and(spare, b_chunk == (group + 2) * per_group - 1))
            def _():
                collect(group)

        return 0

    lax.fori_loop(0, lag + chunks, tick, 0)

    @pl.when(pause_end)
    def _():
        share_whole(2, go)

    def remaining(group, _):
        collect(group)
        return 0

    lax.fori_loop(jnp.where(spare, GROUPS - 1, 0), GROUPS, remaining, 0)
    summed = pdown[...]
    pdown[...] = summed * gain[:, own]
    pgain[...] = jnp.sum(summed * wd_t[:, own].astype(F32), axis=0, keepdims=True)

    def settle(i, _):
        peer = peer_of(i)
        for kind, ref in enumerate((rb_all, act_all, go_all, gi_all)):
            spot = ref.at[:, peer]
            exchange(kind, spot, spot, 0, peer, peer).wait_send()
        return 0

    lax.fori_loop(0, replicas - 1, settle, 0)

    def sent_all(buffer, way, device):
        pltpu.make_async_remote_copy(
            src_ref=buffer, dst_ref=buffer, send_sem=relay_send.at[way], recv_sem=f_recv.at[0, 0],
            device_id=device, device_id_type=MESH,
        ).wait_send()

    @pl.when(jnp.logical_not(last))
    def _():
        sent_all(delta, 0, above)

    @pl.when(jnp.logical_not(first))
    def _():
        sent_all(lim, 1, below)

    pltpu.make_async_copy(base, reb_hbm, out_sem).wait()


def relay_call(sections, replicas, slab, ids, exps, in_table, sent_table, cotangent, w_down, w_up, gain):
    tokens, features = cotangent.shape
    adapter = w_down.shape[1]
    part = features // replicas
    chunks = tokens // RC
    grouped = (GROUPS, replicas, tokens // GROUPS)
    whole = pltpu.VMEM((tokens, features), BF16)
    anywhere = pl.BlockSpec(memory_space=pl.ANY)
    in_vmem = pl.BlockSpec(memory_space=pltpu.VMEM)
    dma = pltpu.SemaphoreType.DMA
    return pl.pallas_call(
        functools.partial(relay_kernel, sections, replicas, slab),
        out_shape=(
            jax.ShapeDtypeStruct((tokens, features), BF16),
            jax.ShapeDtypeStruct((adapter, part), F32),
            jax.ShapeDtypeStruct((adapter, part), F32),
            jax.ShapeDtypeStruct((1, part), F32),
        ),
        in_specs=[pl.BlockSpec(memory_space=pltpu.SMEM)] + [anywhere] * 7,
        out_specs=(anywhere, in_vmem, in_vmem, in_vmem),
        scratch_shapes=[
            pltpu.VMEM(in_table.shape, BF16),
            pltpu.VMEM(sent_table.shape, BF16),
            pltpu.VMEM(exps.shape, jnp.int32),
            pltpu.VMEM((1, features), F32),
            whole, whole, whole, whole, whole,
            pltpu.VMEM((RC, features // PIECES), BF16),
            pltpu.VMEM((features, adapter), BF16),
            pltpu.VMEM((adapter, features), BF16),
            pltpu.VMEM((adapter, features), BF16),
            pltpu.VMEM((features, adapter), BF16),
            pltpu.VMEM(grouped + (part,), BF16),
            pltpu.VMEM(grouped + (part,), BF16),
            pltpu.VMEM(grouped + (adapter,), BF16),
            pltpu.VMEM(grouped + (adapter,), BF16),
            pltpu.VMEM((tokens, adapter), F32),
            pltpu.VMEM((tokens, BLOCK), F32),
            dma((6,)), dma((chunks, PIECES)), dma((chunks, PIECES)), dma((2,)),
            dma((4, replicas)), dma((4, GROUPS, replicas)), dma,
        ],
        compiler_params=pltpu.CompilerParams(
            collective_id=0, has_side_effects=True, vmem_limit_bytes=60 * 2**20
        ),
        cost_estimate=pl.CostEstimate(
            flops=12 * tokens * features * adapter, bytes_accessed=24 * 2**20, transcendentals=0
        ),
        name="relay",
    )(ids, exps, in_table, sent_table, cotangent, w_down, w_up, gain)


def finish_kernel(reb, pdown, pup, pgain, out_reb, grad_down, grad_up, gain_grad):
    out_reb[...] = reb[...]
    grad_down[...] = pdown[...].T
    grad_up[...] = pup[...]
    gain_grad[...] = pgain[...]


def finish(rebuilt, pdown, pup, pgain):
    steps = 2
    (tokens, features), (adapter, part) = rebuilt.shape, pdown.shape
    block = pl.BlockSpec((tokens // steps, features), lambda i: (i, 0))
    across = pl.BlockSpec((adapter, part // steps), lambda i: (0, i))
    down = pl.BlockSpec((part // steps, adapter), lambda i: (i, 0))
    gains = pl.BlockSpec((1, part // steps), lambda i: (0, i))
    return pl.pallas_call(
        finish_kernel,
        out_shape=(
            jax.ShapeDtypeStruct(rebuilt.shape, BF16),
            jax.ShapeDtypeStruct((part, adapter), F32),
            jax.ShapeDtypeStruct(pup.shape, F32),
            jax.ShapeDtypeStruct(pgain.shape, F32),
        ),
        grid=(steps,),
        in_specs=[block, across, across, gains],
        out_specs=(block, down, across, gains),
        compiler_params=pltpu.CompilerParams(vmem_limit_bytes=60 * 2**20),
        name="finish",
    )(rebuilt, pdown, pup, pgain)


def solution(mesh):
    sections, replicas = mesh.shape["section"], mesh.shape["dp"]

    def on_device(in_bases, sent_bases, sample_ids, exponents, cotangent, w_down, w_up, norm_gain):
        micro, rows, features = cotangent.shape[1:]
        flat = (-1, features)
        rebuilt, pdown, pup, pgain = relay_call(
            sections, replicas, rows, sample_ids, exponents[0].reshape(micro * rows, -1),
            in_bases[0, 0].reshape(flat), sent_bases[0, 0].reshape(flat),
            cotangent[0].reshape(flat), w_down[0], w_up[0], norm_gain,
        )
        rebuilt, grad_down, grad_up, gain_grad = finish(rebuilt, pdown, pup, pgain)
        return (
            rebuilt.reshape(1, 1, micro, rows, features),
            grad_down[None],
            grad_up[None],
            gain_grad,
        )

    return jax.shard_map(
        on_device,
        mesh=mesh,
        in_specs=(
            P("section", "dp", None, None, None),
            P("section", "dp", None, None, None),
            P("dp", None),
            P("dp", None, None, None),
            P("dp", None, None, None),
            P("section", None, None),
            P("section", None, None),
            P("section", None),
        ),
        out_specs=(
            P("section", "dp", None, None, None),
            P("section", "dp", None),
            P("section", None, "dp"),
            P("section", "dp"),
        ),
        check_vma=False,
    )
```
